512 devices in a mesh: tensor: 4 (over z_hi, core), row: 8 (over z_lo), col: 16 (over x, y).
Axes of the slice: x: 4, y: 4, z: 16 (z_hi: 2, z_lo: 8; z = z_hi * 8 + z_lo), core: 2. Of those that a mesh axis runs over, the one named last changes fastest.
Arguments:
- features: bfloat16 [16384, 6144], P(('row', 'col'), 'tensor'), may hold values from -8 to 8
- w_proj: bfloat16 [6144, 1024], P('tensor'), may hold values from -0.078125 to 0.078125
- flags: int32 [16384], P(('row', 'col')), may hold values 0 or 1
- rates: float32 [5], replicated, may hold values from 0.25 to 4
Outputs:
- feature_grad: bfloat16 [16384, 6144], P(('row', 'col'), 'tensor')
The draws below stay inside these ranges and needn't reach their ends.
All inputs are finite; a program needn't handle non-finite values. No bound on the sum of `flags` on one device may be relied on, other than what follows from the above.
Results may differ from the reference program's by a relative error of at most 0.029.
Values may be sent and summed in bfloat16 or wider, within the bound.
No kernel may reach another device: no remote copies, remote signals or barrier semaphores. Data moves between devices by JAX's collectives and lax.ppermute only.
A program may use at most 64 MiB of HBM per device.

```python
import math
import jax
import jax.numpy as jnp
from jax import lax

D = 6144
P_SIZE = 1024
NB = 5
GROUP_ROWS = 128
NROWS = 16384
N_TENSOR = 4
N_ROW = 8
N_COL = 16


def draw_features(key, part):
    key = jax.random.fold_in(key, 11)
    key_ids, key_centre, key_noise, key_scale = jax.random.split(key, 4)
    labels = jax.random.randint(key_ids, (NROWS,), 0, 16)
    centres = jax.random.normal(key_centre, (16, D), jnp.float32)
    noise = jax.random.normal(key_noise, (NROWS, D), jnp.float32)
    scale = jnp.exp(jax.random.uniform(key_scale, (NROWS, 1), jnp.float32, -0.35, 0.35))
    values = scale * (0.8 * centres[labels] + 0.6 * noise)
    return jnp.clip(values, -8.0, 8.0).astype(jnp.bfloat16)


def plant(entries, own_key, smallest, largest):
    dims = entries.shape
    place = [jax.random.randint(jax.random.fold_in(own_key, axis), (), 0, dims[axis]) for axis in range(len(dims))]
    entries = entries.at[tuple(place)].set(smallest)
    longest = dims.index(max(dims))
    place[longest] = (place[longest] + 1) % dims[longest]
    return entries.at[tuple(place)].set(largest)


def steps_of(own_key, extent, shards, low, top_value):
    gain, own = 1.0, jax.random.fold_in(own_key, 6)
    for axis_at, shards_of in shards:
        draws = jnp.exp(jax.random.uniform(jax.random.fold_in(own, axis_at), (shards_of,), jnp.float32, low / len(shards), top_value / len(shards)))
        gain = gain * jnp.repeat(draws, extent[axis_at] // shards_of).reshape([-1 if axis == axis_at else 1 for axis in range(len(extent))])
    return gain


def normal_values(stream_key, extent, scale, bound, pieces=(), kind=jnp.bfloat16):
    array = scale * jax.random.normal(stream_key, extent, jnp.float32)
    if pieces:
        array = array * steps_of(stream_key, extent, pieces, -0.22, 0.18)
    return jnp.clip(array, -bound, bound).astype(kind)


def setup_inputs(seed: int = 0) -> dict:
    arg_keys = jax.random.split(jax.random.key(seed), 5)
    return {
        "features": draw_features(jax.random.fold_in(arg_keys[4], 71), 0),
        "w_proj": normal_values(arg_keys[1], (D, P_SIZE), D ** -0.5, 0.078125, ((0, 4),)),
        "flags": plant((jax.random.randint(arg_keys[2], (NROWS,), 0, 2) < 1).astype(jnp.int32), jax.random.fold_in(arg_keys[2], 1), 0, 1),
        "rates": jnp.clip(jnp.exp(jax.random.uniform(arg_keys[3], (NB,), jnp.float32, math.log(0.25), math.log(4.0))), 0.25, 4.0),
    }


def pair_terms(row_z, row_s, col_z, col_s, rates):
    hp = lax.Precision.HIGHEST
    row_norm = jnp.sum(row_z * row_z, axis=1)
    col_norm = jnp.sum(col_z * col_z, axis=1)
    cross = jnp.dot(row_z, col_z.T, precision=hp)
    dist = jnp.maximum(row_norm[:, None] + col_norm[None, :] - 2.0 * cross, 0.0) / P_SIZE
    kernel = jnp.zeros_like(dist)
    for band in range(NB):
        kernel = kernel + rates[band] * jnp.exp(-rates[band] * dist)
    mixed = (-16.0 / P_SIZE) * row_s[:, None] * col_s[None, :] * kernel
    rounded = mixed.astype(jnp.bfloat16).astype(jnp.float32)
    row_part = jnp.sum(mixed, axis=1)[:, None] * row_z - jnp.dot(rounded, col_z, precision=hp)
    col_part = jnp.sum(mixed, axis=0)[:, None] * col_z - jnp.dot(rounded.T, row_z, precision=hp)
    row_part = row_part.astype(jnp.bfloat16).astype(jnp.float32)
    col_part = col_part.astype(jnp.bfloat16).astype(jnp.float32)
    return row_part, col_part


def reference(features, w_proj, flags, rates):
    hp = lax.Precision.HIGHEST
    n_row = N_ROW
    n_col = N_COL
    n_ten = N_TENSOR
    group = GROUP_ROWS
    quarter = group // n_ten
    weights = w_proj.astype(jnp.float32)
    proj = jnp.dot(features.astype(jnp.float32), weights, precision=hp)
    proj = proj.astype(jnp.bfloat16).astype(jnp.float32)
    signs = (1 - 2 * flags).astype(jnp.float32)
    grid_z = proj.reshape(n_row, n_col, group, P_SIZE)
    grid_s = signs.reshape(n_row, n_col, group)
    zero = jnp.int32(0)

    def one_tile(accum, index):
        rpos = (index // (n_col * n_ten)).astype(jnp.int32)
        cpos = ((index // n_ten) % n_col).astype(jnp.int32)
        tpos = (index % n_ten).astype(jnp.int32)
        start = (tpos * quarter).astype(jnp.int32)
        row_z = lax.dynamic_slice(grid_z, (zero, cpos, zero, zero), (n_row, 1, group, P_SIZE)).reshape(n_row * group, P_SIZE)
        row_s = lax.dynamic_slice(grid_s, (zero, cpos, zero), (n_row, 1, group)).reshape(n_row * group)
        col_z = lax.dynamic_slice(grid_z, (rpos, zero, start, zero), (1, n_col, quarter, P_SIZE)).reshape(n_col * quarter, P_SIZE)
        col_s = lax.dynamic_slice(grid_s, (rpos, zero, start), (1, n_col, quarter)).reshape(n_col * quarter)
        row_part, col_part = pair_terms(row_z, row_s, col_z, col_s, rates)
        old = lax.dynamic_slice(accum, (zero, cpos, zero, zero), (n_row, 1, group, P_SIZE))
        accum = lax.dynamic_update_slice(accum, old + row_part.reshape(n_row, 1, group, P_SIZE), (zero, cpos, zero, zero))
        old = lax.dynamic_slice(accum, (rpos, zero, start, zero), (1, n_col, quarter, P_SIZE))
        accum = lax.dynamic_update_slice(accum, old + col_part.reshape(1, n_col, quarter, P_SIZE), (rpos, zero, start, zero))
        return accum, None

    accum = jnp.zeros((n_row, n_col, group, P_SIZE), jnp.float32)
    accum, _ = lax.scan(one_tile, accum, jnp.arange(n_row * n_col * n_ten, dtype=jnp.int32))
    grad_z = accum.reshape(n_row * n_col * group, P_SIZE).astype(jnp.bfloat16).astype(jnp.float32)
    result = jnp.dot(grad_z, weights.T, precision=hp)
    return result.astype(jnp.bfloat16)
```

```python
import jax
import jax.numpy as jnp
from jax import lax
from jax.sharding import PartitionSpec as P

ZLINE = ("tensor", "row")
PAD = 128


def line_permutation(shift, n_row):
    length = 2 * n_row
    pairs = []
    for chip in range(length):
        for core in range(2):
            chip2, core2 = shift(chip, core)
            chip2 %= length
            source = ((chip // n_row) * 2 + core) * n_row + chip % n_row
            target = ((chip2 // n_row) * 2 + core2) * n_row + chip2 % n_row
            pairs.append((source, target))
    return pairs


def pick(second, low, high):
    return jnp.where(second, high, low)


def shards(features, w_proj, flags, rates):
    f32, bf16 = jnp.float32, jnp.bfloat16
    group = features.shape[0]
    width = w_proj.shape[1]
    n_row = lax.axis_size("row")
    n_col = lax.axis_size("col")
    half, quarter = group // 2, group // 4
    tpos = lax.axis_index("tensor")
    high, core = tpos // 2 == 1, tpos % 2 == 1

    def move(value, shift):
        return lax.ppermute(value, ZLINE, line_permutation(shift, n_row))

    def other_core(value):
        return move(value, lambda chip, core: (chip, 1 - core))

    away = pick(core, features[half:], features[:half])
    mine = pick(core, features[:half], features[half:])
    sent = other_core(jnp.dot(away, w_proj, preferred_element_type=f32).astype(bf16))
    kept = jnp.dot(mine, w_proj, preferred_element_type=f32)
    partial = (kept + sent.astype(f32)).astype(bf16)
    far = move(partial, lambda chip, core: (chip + n_row, core))
    z_half = (partial.astype(f32) + far.astype(f32)).astype(bf16)
    signs = (1 - 2 * flags).astype(bf16)
    s_half = pick(core, signs[:half], signs[half:])
    block = jnp.concatenate([z_half, jnp.broadcast_to(s_half[:, None], (half, PAD))], axis=1)

    blocks = [block]
    for shift in range(1, n_row // 2 + 1):
        blocks.append(move(block, lambda chip, core: (chip - shift, core)))
        if shift < n_row // 2:
            blocks.append(move(block, lambda chip, core: (chip + shift, core)))
    own = pick(high, block[:quarter], block[quarter:])
    col = lax.all_to_all(
        jnp.broadcast_to(own[None], (n_col,) + own.shape), "col", 0, 0, tiled=True
    ).reshape(n_col * quarter, width + PAD)
    near = jnp.concatenate(blocks, axis=0)
    rows = jnp.concatenate([near, other_core(near)], axis=0)
    row_z, row_s = rows[:, :width], rows[:, width].astype(f32)
    col_z, col_s = col[:, :width], col[:, width].astype(f32)

    row_norm = jnp.sum(jnp.square(row_z.astype(f32)), axis=1)
    col_norm = jnp.sum(jnp.square(col_z.astype(f32)), axis=1)
    cross = lax.dot_general(col_z, row_z, (((1,), (1,)), ((), ())), preferred_element_type=f32)
    dist = jnp.maximum(col_norm[:, None] + row_norm[None, :] - 2.0 * cross, 0.0) / width
    kernel = jnp.zeros_like(dist)
    for band in range(rates.shape[0]):
        kernel = kernel + rates[band] * jnp.exp(-rates[band] * dist)
    mixed = -16.0 / width * col_s[:, None] * row_s[None, :] * kernel
    total = jnp.sum(mixed, axis=1)
    other = jnp.dot(mixed.astype(bf16), row_z, preferred_element_type=f32)
    part = (2.0 * (total[:, None] * col_z.astype(f32) - other)).astype(bf16)
    parts = lax.all_to_all(part.reshape(n_col, quarter, width), "col", 0, 0, tiled=True)
    grad = jnp.sum(parts.astype(f32), axis=0).astype(bf16)
    grad_far = move(grad, lambda chip, core: (chip + n_row, core))
    grad = pick(
        high, jnp.concatenate([grad, grad_far], axis=0), jnp.concatenate([grad_far, grad], axis=0)
    )
    grad_other = other_core(grad)
    grad = pick(
        core,
        jnp.concatenate([grad, grad_other], axis=0),
        jnp.concatenate([grad_other, grad], axis=0),
    )
    result = lax.dot_general(grad, w_proj, (((1,), (1,)), ((), ())), preferred_element_type=f32)
    return result.astype(bf16)


def solution(mesh):
    in_specs = (P(("row", "col"), "tensor"), P("tensor", None), P(("row", "col")), P())
    out_specs = P(("row", "col"), "tensor")
    return jax.shard_map(shards, mesh=mesh, in_specs=in_specs, out_specs=out_specs, check_vma=False)
```

```python
import functools
import math

import jax
import jax.numpy as jnp
from jax import lax
from jax.experimental import pallas as pl
from jax.experimental.pallas import tpu as pltpu
from jax.sharding import PartitionSpec as P

ZLINE = ("tensor", "row")
PAD = 128
LOG2E = math.log2(math.e)


def line_permutation(shift, n_row):
    length = 2 * n_row
    pairs = []
    for chip in range(length):
        for core in range(2):
            chip2, core2 = shift(chip, core)
            chip2 %= length
            source = ((chip // n_row) * 2 + core) * n_row + chip % n_row
            target = ((chip2 // n_row) * 2 + core2) * n_row + chip2 % n_row
            pairs.append((source, target))
    return pairs


def pick(second, low, high):
    return jnp.where(second, high, low)

def tile_kernel(count, *refs):
    f32, bf16 = jnp.float32, jnp.bfloat16
    rates_ref, col_ref = refs[:2]
    pieces, refs = refs[2 : 2 + count], refs[2 + count :]
    last = len(refs) == 5
    held, refs = (refs[:2], refs[2:]) if last else (None, refs)
    outs, (rows_ref, signed_ref) = refs[:-2], refs[-2:]
    width = col_ref.shape[1] - PAD
    depth = pieces[0].shape[0]
    n_rows = count * depth

    turned = []
    for index, piece in enumerate(pieces):
        place = slice(index * depth, (index + 1) * depth)
        sign = piece[:, width:]
        square = jnp.zeros((depth, PAD), f32)
        for at in range(0, width, PAD):
            part = piece[:, at : at + PAD]
            rows_ref[place, at : at + PAD] = part
            signed_ref[place, at : at + PAD] = part * sign
            square += jnp.square(part.astype(f32))
        norm = jnp.sum(square, axis=1, keepdims=True)
        lane = lax.broadcasted_iota(jnp.int32, (depth, PAD), 1)
        turned.append(jnp.where(lane == 0, norm, sign.astype(f32)).T)
    row_norm = jnp.concatenate([value[0:1] for value in turned], axis=1)
    row_sign = jnp.concatenate([value[1:2] for value in turned], axis=1)

    scales = [rates_ref[band] * (-LOG2E / width) for band in range(rates_ref.shape[0])]
    step = min(128, col_ref.shape[0])
    for start in range(0, col_ref.shape[0], step):
        place = slice(start, start + step)
        col_z = col_ref[place, :width]
        wide = col_z.astype(f32)
        col_norm = jnp.sum(jnp.square(wide), axis=1, keepdims=True)
        cross = lax.dot_general(
            col_z, rows_ref[...], (((1,), (1,)), ((), ())), preferred_element_type=f32
        )
        dist = jnp.maximum(col_norm + row_norm - 2.0 * cross, 0.0)
        kernel = jnp.zeros((step, n_rows), f32)
        for band, scale in enumerate(scales):
            kernel += rates_ref[band] * jnp.exp2(scale * dist)
        total = jnp.broadcast_to(jnp.sum(kernel * row_sign, axis=1, keepdims=True), (step, PAD))
        other = jnp.dot(kernel.astype(bf16), signed_ref[...], preferred_element_type=f32)
        if last:
            total += held[0][place]
            other += held[1][place]
            factor = (-32.0 / width) * col_ref[place, width : width + 1].astype(f32)
            outs[0][place] = (factor * (total[:, :1] * wide - other)).astype(bf16)
        else:
            outs[0][place] = total
            outs[1][place] = other


def tiles(pieces, col, rates, held=()):
    f32, bf16 = jnp.float32, jnp.bfloat16
    n_cols, width = col.shape[0], col.shape[1] - PAD
    n_rows = sum(piece.shape[0] for piece in pieces)
    vmem = pl.BlockSpec(memory_space=pltpu.VMEM)
    if held:
        out_shape = jax.ShapeDtypeStruct((n_cols, width), bf16)
    else:
        out_shape = (
            jax.ShapeDtypeStruct((n_cols, PAD), f32),
            jax.ShapeDtypeStruct((n_cols, width), f32),
        )
    pairs = n_rows * n_cols
    return pl.pallas_call(
        functools.partial(tile_kernel, len(pieces)),
        out_shape=out_shape,
        in_specs=[pl.BlockSpec(memory_space=pltpu.SMEM)] + [vmem] * (1 + len(pieces) + len(held)),
        out_specs=vmem if held else (vmem, vmem),
        scratch_shapes=[pltpu.VMEM((n_rows, width), bf16), pltpu.VMEM((n_rows, width), bf16)],
        compiler_params=pltpu.CompilerParams(vmem_limit_bytes=32 * 2**20),
        cost_estimate=pl.CostEstimate(
            flops=4 * pairs * width, bytes_accessed=4 * n_cols * width, transcendentals=5 * pairs
        ),
    )(rates, col, *pieces, *held)


def shards(features, w_proj, flags, rates):
    f32, bf16 = jnp.float32, jnp.bfloat16
    group = features.shape[0]
    width = w_proj.shape[1]
    n_row = lax.axis_size("row")
    n_col = lax.axis_size("col")
    half, quarter = group // 2, group // 4
    tpos = lax.axis_index("tensor")
    high, core = tpos // 2 == 1, tpos % 2 == 1

    def move(value, shift):
        return lax.ppermute(value, ZLINE, line_permutation(shift, n_row))

    def other_core(value):
        return move(value, lambda chip, core: (chip, 1 - core))

    away = pick(core, features[half:], features[:half])
    mine = pick(core, features[:half], features[half:])
    sent = other_core(jnp.dot(away, w_proj, preferred_element_type=f32).astype(bf16))
    kept = jnp.dot(mine, w_proj, preferred_element_type=f32)
    partial = (kept + sent.astype(f32)).astype(bf16)
    far = move(partial, lambda chip, core: (chip + n_row, core))
    z_half = (partial.astype(f32) + far.astype(f32)).astype(bf16)
    signs = (1 - 2 * flags).astype(bf16)
    s_half = pick(core, signs[:half], signs[half:])
    block = jnp.concatenate([z_half, jnp.broadcast_to(s_half[:, None], (half, PAD))], axis=1)

    far_block = move(block, lambda chip, core: (chip + (n_row // 2) * (1 - 2 * core), core))
    pair = jnp.concatenate([block, far_block], axis=0)
    near = [
        pair,
        move(pair, lambda chip, core: (chip + 1, core)),
        move(pair, lambda chip, core: (chip - 1, core)),
        move(pair, lambda chip, core: (chip + 2 - 4 * core, core)),
    ]
    own = pick(high, block[:quarter], block[quarter:])
    col = lax.all_to_all(
        jnp.broadcast_to(own[None], (n_col,) + own.shape), "col", 0, 0, tiled=True
    ).reshape(n_col * quarter, width + PAD)
    sums = tiles(near, col, rates)
    part = tiles([other_core(value) for value in near], col, rates, sums)
    parts = lax.all_to_all(part.reshape(n_col, quarter, width), "col", 0, 0, tiled=True)
    grad = jnp.sum(parts.astype(f32), axis=0).astype(bf16)
    grad_far = move(grad, lambda chip, core: (chip + n_row, core))
    grad = pick(
        high, jnp.concatenate([grad, grad_far], axis=0), jnp.concatenate([grad_far, grad], axis=0)
    )
    grad_other = other_core(grad)
    grad = pick(
        core,
        jnp.concatenate([grad, grad_other], axis=0),
        jnp.concatenate([grad_other, grad], axis=0),
    )
    result = lax.dot_general(grad, w_proj, (((1,), (1,)), ((), ())), preferred_element_type=f32)
    return result.astype(bf16)


def solution(mesh):
    in_specs = (P(("row", "col"), "tensor"), P("tensor", None), P(("row", "col")), P())
    out_specs = P(("row", "col"), "tensor")
    return jax.shard_map(shards, mesh=mesh, in_specs=in_specs, out_specs=out_specs, check_vma=False)
```

```python
import functools
import math

import jax
import jax.numpy as jnp
from jax import lax
from jax.experimental import pallas as pl
from jax.experimental.pallas import tpu as pltpu
from jax.sharding import PartitionSpec as P

ZLINE = ("tensor", "row")
PAD = 128
LOG2E = math.log2(math.e)
FLOPS = 4 * 10**10


def line_permutation(shift, n_row):
    length = 2 * n_row
    pairs = []
    for chip in range(length):
        for core in range(2):
            chip2, core2 = shift(chip, core)
            chip2 %= length
            source = ((chip // n_row) * 2 + core) * n_row + chip % n_row
            target = ((chip2 // n_row) * 2 + core2) * n_row + chip2 % n_row
            pairs.append((source, target))
    return pairs


def pick(second, low, high):
    return jnp.where(second, high, low)

CHUNKS = 4


def projection_kernel(core_ref, features_ref, w_ref, away_ref, kept_ref, rows, weights, total, sem):
    copies = []
    depth = rows.shape[1] // CHUNKS
    for index in range(CHUNKS):
        place = pl.ds(index * depth, depth)
        copies.append(
            (
                pltpu.make_async_copy(features_ref.at[:, place], rows.at[:, place], sem.at[0, index]),
                pltpu.make_async_copy(w_ref.at[place], weights.at[place], sem.at[1, index]),
            )
        )
        for copy in copies[-1]:
            copy.start()
    value = None
    for index in range(CHUNKS):
        place = slice(index * depth, (index + 1) * depth)
        for copy in copies[index]:
            copy.wait()
        term = jnp.dot(rows[:, place], weights[place], preferred_element_type=jnp.float32)
        value = term if value is None else value + term
    total[...] = value
    half = kept_ref.shape[0]
    core = core_ref[0]
    away = total[pl.ds(pl.multiple_of((1 - core) * half, half), half)]
    away_ref[...] = away.astype(away_ref.dtype)
    kept_ref[...] = total[pl.ds(pl.multiple_of(core * half, half), half)]


def projection(core, features, w_proj):
    rows, width = features.shape[0], w_proj.shape[1]
    vmem, anywhere = pl.BlockSpec(memory_space=pltpu.VMEM), pl.BlockSpec(memory_space=pl.ANY)
    return pl.pallas_call(
        projection_kernel,
        out_shape=(
            jax.ShapeDtypeStruct((rows // 2, width), jnp.bfloat16),
            jax.ShapeDtypeStruct((rows // 2, width), jnp.float32),
        ),
        in_specs=[pl.BlockSpec(memory_space=pltpu.SMEM), anywhere, anywhere],
        out_specs=(vmem, vmem),
        scratch_shapes=[
            pltpu.VMEM(features.shape, features.dtype),
            pltpu.VMEM(w_proj.shape, w_proj.dtype),
            pltpu.VMEM((rows, width), jnp.float32),
            pltpu.SemaphoreType.DMA((2, CHUNKS)),
        ],
        compiler_params=pltpu.CompilerParams(vmem_limit_bytes=60 * 2**20),
        cost_estimate=pl.CostEstimate(
            flops=2 * rows * width * w_proj.shape[0],
            bytes_accessed=2 * w_proj.shape[0] * width,
            transcendentals=0,
        ),
    )(core, features, w_proj)


def pair_kernel(first_ref, second_ref, out_ref):
    half = first_ref.shape[0]
    out_ref[:half] = first_ref[...]
    out_ref[half:] = second_ref[...]


def side_by_side(first, second):
    vmem = pl.BlockSpec(memory_space=pltpu.VMEM)
    return pl.pallas_call(
        pair_kernel,
        out_shape=jax.ShapeDtypeStruct((2 * first.shape[0], first.shape[1]), first.dtype),
        in_specs=[vmem, vmem],
        out_specs=vmem,
        compiler_params=pltpu.CompilerParams(vmem_limit_bytes=16 * 2**20),
        cost_estimate=pl.CostEstimate(flops=FLOPS, bytes_accessed=0, transcendentals=0),
    )(first, second)


def tile_kernel(count, *refs):
    f32, bf16 = jnp.float32, jnp.bfloat16
    rates_ref, col_ref = refs[:2]
    pieces, refs = refs[2 : 2 + count], refs[2 + count :]
    last = len(refs) == 5
    held, refs = (refs[:2], refs[2:]) if last else (None, refs)
    outs, (rows_ref, signed_ref) = refs[:-2], refs[-2:]
    width = col_ref.shape[1] - PAD
    depth = pieces[0].shape[0]
    n_rows = count * depth

    turned = []
    for index, piece in enumerate(pieces):
        place = slice(index * depth, (index + 1) * depth)
        sign = piece[:, width:]
        square = jnp.zeros((depth, PAD), f32)
        for at in range(0, width, PAD):
            part = piece[:, at : at + PAD]
            rows_ref[place, at : at + PAD] = part
            signed_ref[place, at : at + PAD] = part * sign
            square += jnp.square(part.astype(f32))
        norm = jnp.sum(square, axis=1, keepdims=True)
        lane = lax.broadcasted_iota(jnp.int32, (depth, PAD), 1)
        turned.append(jnp.where(lane == 0, norm, sign.astype(f32)).T)
    row_norm = jnp.concatenate([value[0:1] for value in turned], axis=1)
    row_sign = jnp.concatenate([value[1:2] for value in turned], axis=1)

    scales = [rates_ref[band] * (-LOG2E / width) for band in range(rates_ref.shape[0])]
    step = min(256, col_ref.shape[0])
    for start in range(0, col_ref.shape[0], step):
        place = slice(start, start + step)
        col_z = col_ref[place, :width]
        wide = col_z.astype(f32)
        col_norm = jnp.sum(jnp.square(wide), axis=1, keepdims=True)
        cross = lax.dot_general(
            col_z, rows_ref[...], (((1,), (1,)), ((), ())), preferred_element_type=f32
        )
        dist = jnp.maximum(col_norm + row_norm - 2.0 * cross, 0.0)
        kernel = jnp.zeros((step, n_rows), f32)
        for band, scale in enumerate(scales):
            kernel += rates_ref[band] * jnp.exp2(scale * dist)
        total = jnp.broadcast_to(jnp.sum(kernel * row_sign, axis=1, keepdims=True), (step, PAD))
        other = jnp.dot(kernel.astype(bf16), signed_ref[...], preferred_element_type=f32)
        if last:
            total += held[0][place]
            other += held[1][place]
            factor = (-32.0 / width) * col_ref[place, width : width + 1].astype(f32)
            outs[0][place] = (factor * (total[:, :1] * wide - other)).astype(bf16)
        else:
            outs[0][place] = total
            outs[1][place] = other


def tiles(pieces, col, rates, held=()):
    f32, bf16 = jnp.float32, jnp.bfloat16
    n_cols, width = col.shape[0], col.shape[1] - PAD
    n_rows = sum(piece.shape[0] for piece in pieces)
    vmem = pl.BlockSpec(memory_space=pltpu.VMEM)
    if held:
        out_shape = jax.ShapeDtypeStruct((n_cols, width), bf16)
    else:
        out_shape = (
            jax.ShapeDtypeStruct((n_cols, PAD), f32),
            jax.ShapeDtypeStruct((n_cols, width), f32),
        )
    pairs = n_rows * n_cols
    return pl.pallas_call(
        functools.partial(tile_kernel, len(pieces)),
        out_shape=out_shape,
        in_specs=[pl.BlockSpec(memory_space=pltpu.SMEM)] + [vmem] * (1 + len(pieces) + len(held)),
        out_specs=vmem if held else (vmem, vmem),
        scratch_shapes=[pltpu.VMEM((n_rows, width), bf16), pltpu.VMEM((n_rows, width), bf16)],
        compiler_params=pltpu.CompilerParams(vmem_limit_bytes=32 * 2**20),
        cost_estimate=pl.CostEstimate(
            flops=4 * pairs * width, bytes_accessed=4 * n_cols * width, transcendentals=5 * pairs
        ),
    )(rates, col, *pieces, *held)


def shards(features, w_proj, flags, rates):
    f32, bf16 = jnp.float32, jnp.bfloat16
    group = features.shape[0]
    width = w_proj.shape[1]
    n_row = lax.axis_size("row")
    n_col = lax.axis_size("col")
    half, quarter = group // 2, group // 4
    tpos = lax.axis_index("tensor")
    high, core = tpos // 2 == 1, tpos % 2 == 1

    def move(value, shift):
        return lax.ppermute(value, ZLINE, line_permutation(shift, n_row))

    def other_core(value):
        return move(value, lambda chip, core: (chip, 1 - core))

    away, kept = projection(jnp.reshape(tpos % 2, (1,)), features, w_proj)
    partial = (kept + other_core(away).astype(f32)).astype(bf16)
    far = move(partial, lambda chip, core: (chip + n_row, core))
    z_half = (partial.astype(f32) + far.astype(f32)).astype(bf16)
    signs = (1 - 2 * flags).astype(bf16)
    s_half = pick(core, signs[:half], signs[half:])
    block = jnp.concatenate([z_half, jnp.broadcast_to(s_half[:, None], (half, PAD))], axis=1)

    far_block = move(block, lambda chip, core: (chip + (n_row // 2) * (1 - 2 * core), core))
    pair = side_by_side(block, far_block)
    near = [
        pair,
        move(pair, lambda chip, core: (chip + 1, core)),
        move(pair, lambda chip, core: (chip - 1, core)),
        move(pair, lambda chip, core: (chip + 2 - 4 * core, core)),
    ]
    own = pick(high, block[:quarter], block[quarter:])
    col = lax.all_to_all(
        jnp.broadcast_to(own[None], (n_col,) + own.shape), "col", 0, 0, tiled=True
    ).reshape(n_col * quarter, width + PAD)
    sums = tiles(near, col, rates)
    part = tiles([other_core(value) for value in near], col, rates, sums)
    parts = lax.all_to_all(part.reshape(n_col, quarter, width), "col", 0, 0, tiled=True)
    grad = jnp.sum(parts.astype(f32), axis=0).astype(bf16)
    grad_far = move(grad, lambda chip, core: (chip + n_row, core))
    grad = pick(
        high, jnp.concatenate([grad, grad_far], axis=0), jnp.concatenate([grad_far, grad], axis=0)
    )
    grad_other = other_core(grad)
    grad = pick(
        core,
        jnp.concatenate([grad, grad_other], axis=0),
        jnp.concatenate([grad_other, grad], axis=0),
    )
    result = lax.dot_general(grad, w_proj, (((1,), (1,)), ((), ())), preferred_element_type=f32)
    return result.astype(bf16)


def solution(mesh):
    in_specs = (P(("row", "col"), "tensor"), P("tensor", None), P(("row", "col")), P())
    out_specs = P(("row", "col"), "tensor")
    return jax.shard_map(shards, mesh=mesh, in_specs=in_specs, out_specs=out_specs, check_vma=False)
```

```python
import functools
import math

import jax
import jax.numpy as jnp
from jax import lax
from jax.experimental import pallas as pl
from jax.experimental.pallas import tpu as pltpu
from jax.sharding import PartitionSpec as P

ZLINE = ("tensor", "row")
PAD = 128
LOG2E = math.log2(math.e)
FLOPS = 4 * 10**10


def line_permutation(shift, n_row):
    length = 2 * n_row
    pairs = []
    for chip in range(length):
        for core in range(2):
            chip2, core2 = shift(chip, core)
            chip2 %= length
            source = ((chip // n_row) * 2 + core) * n_row + chip % n_row
            target = ((chip2 // n_row) * 2 + core2) * n_row + chip2 % n_row
            pairs.append((source, target))
    return pairs


def pick(second, low, high):
    return jnp.where(second, high, low)

CHUNKS = 4


def projection_kernel(core_ref, features_ref, w_ref, away_ref, kept_ref, rows, weights, total, sem):
    copies = []
    depth = rows.shape[1] // CHUNKS
    for index in range(CHUNKS):
        place = pl.ds(index * depth, depth)
        copies.append(
            (
                pltpu.make_async_copy(features_ref.at[:, place], rows.at[:, place], sem.at[0, index]),
                pltpu.make_async_copy(w_ref.at[place], weights.at[place], sem.at[1, index]),
            )
        )
        for copy in copies[-1]:
            copy.start()
    value = None
    for index in range(CHUNKS):
        place = slice(index * depth, (index + 1) * depth)
        for copy in copies[index]:
            copy.wait()
        term = jnp.dot(rows[:, place], weights[place], preferred_element_type=jnp.float32)
        value = term if value is None else value + term
    total[...] = value
    half = kept_ref.shape[0]
    core = core_ref[0]
    away = total[pl.ds(pl.multiple_of((1 - core) * half, half), half)]
    away_ref[...] = away.astype(away_ref.dtype)
    kept_ref[...] = total[pl.ds(pl.multiple_of(core * half, half), half)]


def projection(core, features, w_proj):
    rows, width = features.shape[0], w_proj.shape[1]
    vmem, anywhere = pl.BlockSpec(memory_space=pltpu.VMEM), pl.BlockSpec(memory_space=pl.ANY)
    return pl.pallas_call(
        projection_kernel,
        out_shape=(
            jax.ShapeDtypeStruct((rows // 2, width), jnp.bfloat16),
            jax.ShapeDtypeStruct((rows // 2, width), jnp.float32),
        ),
        in_specs=[pl.BlockSpec(memory_space=pltpu.SMEM), anywhere, anywhere],
        out_specs=(vmem, vmem),
        scratch_shapes=[
            pltpu.VMEM(features.shape, features.dtype),
            pltpu.VMEM(w_proj.shape, w_proj.dtype),
            pltpu.VMEM((rows, width), jnp.float32),
            pltpu.SemaphoreType.DMA((2, CHUNKS)),
        ],
        compiler_params=pltpu.CompilerParams(vmem_limit_bytes=60 * 2**20),
        cost_estimate=pl.CostEstimate(
            flops=2 * rows * width * w_proj.shape[0],
            bytes_accessed=2 * w_proj.shape[0] * width,
            transcendentals=0,
        ),
    )(core, features, w_proj)


def block_kernel(near_ref, far_ref, signs_ref, block_ref):
    f32, bf16 = jnp.float32, jnp.bfloat16
    half, width = near_ref.shape
    rows = (near_ref[...].astype(f32) + far_ref[...].astype(f32)).astype(bf16)
    block_ref[:, :width] = rows
    norm = jnp.sum(jnp.square(rows.astype(f32)), axis=1, keepdims=True)
    first = norm.astype(bf16).astype(f32)
    second = (norm - first).astype(bf16).astype(f32)
    third = norm - first - second
    lane = lax.broadcasted_iota(jnp.int32, (half, PAD), 1)
    tail = jnp.where(lane == 1, first, jnp.where(lane == 2, second, third))
    block_ref[:, width:] = jnp.where(lane == 0, signs_ref[...], tail).astype(bf16)


def whole_block(near, far, signs):
    vmem = pl.BlockSpec(memory_space=pltpu.VMEM)
    half, width = near.shape
    return pl.pallas_call(
        block_kernel,
        out_shape=jax.ShapeDtypeStruct((half, width + PAD), near.dtype),
        in_specs=[vmem] * 3,
        out_specs=vmem,
        compiler_params=pltpu.CompilerParams(vmem_limit_bytes=16 * 2**20),
        cost_estimate=pl.CostEstimate(
            flops=4 * half * width, bytes_accessed=6 * half * width, transcendentals=0
        ),
    )(near, far, signs)


def result_kernel(grad_ref, w_ref, out_ref):
    out_ref[...] = lax.dot_general(
        grad_ref[...], w_ref[...], (((1,), (1,)), ((), ())), preferred_element_type=jnp.float32
    ).astype(out_ref.dtype)


def result(grad, w_proj):
    vmem = pl.BlockSpec(memory_space=pltpu.VMEM)
    rows, depth = grad.shape[0], w_proj.shape[0]
    return pl.pallas_call(
        result_kernel,
        out_shape=jax.ShapeDtypeStruct((rows, depth), grad.dtype),
        in_specs=[vmem] * 2,
        out_specs=vmem,
        compiler_params=pltpu.CompilerParams(vmem_limit_bytes=16 * 2**20),
        cost_estimate=pl.CostEstimate(
            flops=2 * rows * w_proj.size, bytes_accessed=2 * w_proj.size, transcendentals=0
        ),
    )(grad, w_proj)


def pair_kernel(first_ref, second_ref, out_ref):
    half = first_ref.shape[0]
    out_ref[:half] = first_ref[...]
    out_ref[half:] = second_ref[...]


def side_by_side(first, second, flops):
    vmem = pl.BlockSpec(memory_space=pltpu.VMEM)
    return pl.pallas_call(
        pair_kernel,
        out_shape=jax.ShapeDtypeStruct((2 * first.shape[0], first.shape[1]), first.dtype),
        in_specs=[vmem, vmem],
        out_specs=vmem,
        compiler_params=pltpu.CompilerParams(vmem_limit_bytes=16 * 2**20),
        cost_estimate=pl.CostEstimate(flops=flops, bytes_accessed=0, transcendentals=0),
    )(first, second)


def after_kernel(value_ref, first_ref, same_ref):
    pass


def after(value, first):
    anywhere = pl.BlockSpec(memory_space=pl.ANY)
    return pl.pallas_call(
        after_kernel,
        out_shape=jax.ShapeDtypeStruct(value.shape, value.dtype),
        in_specs=[anywhere, anywhere],
        out_specs=anywhere,
        input_output_aliases={0: 0},
        compiler_params=pltpu.CompilerParams(vmem_limit_bytes=16 * 2**20),
        cost_estimate=pl.CostEstimate(flops=0, bytes_accessed=0, transcendentals=0),
    )(value, first)


def tile_kernel(count, more, last, *refs):
    f32, bf16 = jnp.float32, jnp.bfloat16
    rates_ref, col_ref = refs[:2]
    pieces, refs = refs[2 : 2 + count], refs[2 + count :]
    held, refs = (refs[:2], refs[2:]) if more else (None, refs)
    outs, rows_ref = refs[:-1], refs[-1]
    width = col_ref.shape[1] - PAD
    n_rows = rows_ref.shape[0]

    turned, filled = [], 0
    for piece in pieces:
        rows_ref[filled : filled + piece.shape[0]] = piece[:, :width]
        filled += piece.shape[0]
        turned.append(piece[:, width:].astype(f32).T)
    turned = jnp.concatenate([value[:8] for value in turned], axis=1)
    row_sign = turned[0:1]
    row_norm = turned[1:2] + turned[2:3] + turned[3:4]

    scales = [rates_ref[band] * (-LOG2E / width) for band in range(rates_ref.shape[0])]
    step = min(256, col_ref.shape[0])
    for start in range(0, col_ref.shape[0], step):
        place = slice(start, start + step)
        col_z = col_ref[place, :width]
        tail = col_ref[place, width:].astype(f32)
        col_norm = tail[:, 1:2] + tail[:, 2:3] + tail[:, 3:4]
        cross = lax.dot_general(
            col_z, rows_ref[...], (((1,), (1,)), ((), ())), preferred_element_type=f32
        )
        dist = jnp.maximum(col_norm + row_norm - 2.0 * cross, 0.0)
        kernel = jnp.zeros((step, n_rows), f32)
        for band, scale in enumerate(scales):
            kernel += rates_ref[band] * jnp.exp2(scale * dist)
        kernel *= row_sign
        total = jnp.broadcast_to(jnp.sum(kernel, axis=1, keepdims=True), (step, PAD))
        other = jnp.dot(kernel.astype(bf16), rows_ref[...], preferred_element_type=f32)
        if more:
            total += held[0][place]
            other += held[1][place]
        if last:
            factor = (-32.0 / width) * tail[:, 0:1]
            wide = col_z.astype(f32)
            outs[0][place] = (factor * (total[:, :1] * wide - other)).astype(bf16)
        else:
            outs[0][place] = total
            outs[1][place] = other


def tiles(pieces, col, rates, held=(), last=False):
    f32, bf16 = jnp.float32, jnp.bfloat16
    n_cols, width = col.shape[0], col.shape[1] - PAD
    n_rows = sum(piece.shape[0] for piece in pieces)
    vmem = pl.BlockSpec(memory_space=pltpu.VMEM)
    if last:
        out_shape = jax.ShapeDtypeStruct((n_cols, width), bf16)
    else:
        out_shape = (
            jax.ShapeDtypeStruct((n_cols, PAD), f32),
            jax.ShapeDtypeStruct((n_cols, width), f32),
        )
    pairs = n_rows * n_cols
    return pl.pallas_call(
        functools.partial(tile_kernel, len(pieces), bool(held), last),
        out_shape=out_shape,
        in_specs=[pl.BlockSpec(memory_space=pltpu.SMEM)] + [vmem] * (1 + len(pieces) + len(held)),
        out_specs=vmem if last else (vmem, vmem),
        scratch_shapes=[pltpu.VMEM((n_rows, width), bf16)],
        compiler_params=pltpu.CompilerParams(vmem_limit_bytes=32 * 2**20),
        cost_estimate=pl.CostEstimate(
            flops=4 * pairs * width, bytes_accessed=4 * n_cols * width, transcendentals=5 * pairs
        ),
    )(rates, col, *pieces, *held)


def shards(features, w_proj, flags, rates):
    f32, bf16 = jnp.float32, jnp.bfloat16
    group = features.shape[0]
    width = w_proj.shape[1]
    n_row = lax.axis_size("row")
    n_col = lax.axis_size("col")
    half, quarter = group // 2, group // 4
    tpos = lax.axis_index("tensor")
    high, core = tpos // 2 == 1, tpos % 2 == 1

    def move(value, shift):
        return lax.ppermute(value, ZLINE, line_permutation(shift, n_row))

    def other_core(value):
        return move(value, lambda chip, core: (chip, 1 - core))

    away, kept = projection(jnp.reshape(tpos % 2, (1,)), features, w_proj)
    partial = (kept + other_core(away).astype(f32)).astype(bf16)
    far = move(partial, lambda chip, core: (chip + n_row, core))
    signs = (1 - 2 * flags).astype(f32)
    s_half = pick(core, signs[:half], signs[half:])
    block = whole_block(partial, far, jnp.broadcast_to(s_half[:, None], (half, PAD)))

    far_block = move(block, lambda chip, core: (chip + (n_row // 2) * (1 - 2 * core), core))
    pair = side_by_side(block, far_block, FLOPS)
    two_away = move(pair, lambda chip, core: (chip + 2 - 4 * core, core))
    other_pair = other_core(pair)
    one_away = move(
        side_by_side(pair, other_pair, 0), lambda chip, core: (chip + 1 - 2 * core, core)
    )
    own = pick(high, block[:quarter], block[quarter:])
    col = lax.all_to_all(
        jnp.broadcast_to(own[None], (n_col,) + own.shape), "col", 0, 0, tiled=True
    ).reshape(n_col * quarter, width + PAD)
    sums = tiles([pair, other_pair], col, rates)
    one_away = after(one_away, sums[0])
    sums = tiles([two_away, other_core(two_away)], col, rates, sums, False)
    part = tiles([one_away, other_core(one_away)], col, rates, sums, True)
    parts = lax.all_to_all(part.reshape(n_col, quarter, width), "col", 0, 0, tiled=True)
    grad = jnp.sum(parts.astype(f32), axis=0).astype(bf16)
    grad_far = move(grad, lambda chip, core: (chip + n_row, core))
    grad = pick(
        high, jnp.concatenate([grad, grad_far], axis=0), jnp.concatenate([grad_far, grad], axis=0)
    )
    grad_other = other_core(grad)
    grad = pick(
        core,
        jnp.concatenate([grad, grad_other], axis=0),
        jnp.concatenate([grad_other, grad], axis=0),
    )
    return result(grad, w_proj)


def solution(mesh):
    in_specs = (P(("row", "col"), "tensor"), P("tensor", None), P(("row", "col")), P())
    out_specs = P(("row", "col"), "tensor")
    return jax.shard_map(shards, mesh=mesh, in_specs=in_specs, out_specs=out_specs, check_vma=False)
```

```python
import functools
import math

import jax
import jax.numpy as jnp
from jax import lax
from jax.experimental import pallas as pl
from jax.experimental.pallas import tpu as pltpu
from jax.sharding import PartitionSpec as P

ZLINE = ("tensor", "row")
PAD = 128
LOG2E = math.log2(math.e)
FLOPS = 4 * 10**10


def line_permutation(shift, n_row):
    length = 2 * n_row
    pairs = []
    for chip in range(length):
        for core in range(2):
            chip2, core2 = shift(chip, core)
            chip2 %= length
            source = ((chip // n_row) * 2 + core) * n_row + chip % n_row
            target = ((chip2 // n_row) * 2 + core2) * n_row + chip2 % n_row
            pairs.append((source, target))
    return pairs


def pick(second, low, high):
    return jnp.where(second, high, low)

CHUNKS = 4


def projection_kernel(core_ref, features_ref, w_ref, away_ref, kept_ref, rows, weights, total, sem):
    copies = []
    depth = rows.shape[1] // CHUNKS
    for index in range(CHUNKS):
        place = pl.ds(index * depth, depth)
        copies.append(
            (
                pltpu.make_async_copy(features_ref.at[:, place], rows.at[:, place], sem.at[0, index]),
                pltpu.make_async_copy(w_ref.at[place], weights.at[place], sem.at[1, index]),
            )
        )
        for copy in copies[-1]:
            copy.start()
    value = None
    for index in range(CHUNKS):
        place = slice(index * depth, (index + 1) * depth)
        for copy in copies[index]:
            copy.wait()
        term = jnp.dot(rows[:, place], weights[place], preferred_element_type=jnp.float32)
        value = term if value is None else value + term
    total[...] = value
    half = kept_ref.shape[0]
    core = core_ref[0]
    away = total[pl.ds(pl.multiple_of((1 - core) * half, half), half)]
    away_ref[...] = away.astype(away_ref.dtype)
    kept_ref[...] = total[pl.ds(pl.multiple_of(core * half, half), half)]


def projection(core, features, w_proj):
    rows, width = features.shape[0], w_proj.shape[1]
    vmem, anywhere = pl.BlockSpec(memory_space=pltpu.VMEM), pl.BlockSpec(memory_space=pl.ANY)
    return pl.pallas_call(
        projection_kernel,
        out_shape=(
            jax.ShapeDtypeStruct((rows // 2, width), jnp.bfloat16),
            jax.ShapeDtypeStruct((rows // 2, width), jnp.float32),
        ),
        in_specs=[pl.BlockSpec(memory_space=pltpu.SMEM), anywhere, anywhere],
        out_specs=(vmem, vmem),
        scratch_shapes=[
            pltpu.VMEM(features.shape, features.dtype),
            pltpu.VMEM(w_proj.shape, w_proj.dtype),
            pltpu.VMEM((rows, width), jnp.float32),
            pltpu.SemaphoreType.DMA((2, CHUNKS)),
        ],
        compiler_params=pltpu.CompilerParams(vmem_limit_bytes=60 * 2**20),
        cost_estimate=pl.CostEstimate(
            flops=2 * rows * width * w_proj.shape[0],
            bytes_accessed=2 * w_proj.shape[0] * width,
            transcendentals=0,
        ),
    )(core, features, w_proj)


def block_kernel(near_ref, far_ref, signs_ref, block_ref):
    f32, bf16 = jnp.float32, jnp.bfloat16
    half, width = near_ref.shape
    rows = (near_ref[...].astype(f32) + far_ref[...].astype(f32)).astype(bf16)
    block_ref[:, :width] = rows
    norm = jnp.sum(jnp.square(rows.astype(f32)), axis=1, keepdims=True)
    first = norm.astype(bf16).astype(f32)
    second = (norm - first).astype(bf16).astype(f32)
    third = norm - first - second
    lane = lax.broadcasted_iota(jnp.int32, (half, PAD), 1)
    tail = jnp.where(lane == 1, first, jnp.where(lane == 2, second, third))
    block_ref[:, width:] = jnp.where(lane == 0, signs_ref[...], tail).astype(bf16)


def whole_block(near, far, signs):
    vmem = pl.BlockSpec(memory_space=pltpu.VMEM)
    half, width = near.shape
    return pl.pallas_call(
        block_kernel,
        out_shape=jax.ShapeDtypeStruct((half, width + PAD), near.dtype),
        in_specs=[vmem] * 3,
        out_specs=vmem,
        compiler_params=pltpu.CompilerParams(vmem_limit_bytes=16 * 2**20),
        cost_estimate=pl.CostEstimate(
            flops=4 * half * width, bytes_accessed=6 * half * width, transcendentals=0
        ),
    )(near, far, signs)


def result_kernel(grad_ref, w_ref, out_ref):
    out_ref[...] = lax.dot_general(
        grad_ref[...], w_ref[...], (((1,), (1,)), ((), ())), preferred_element_type=jnp.float32
    ).astype(out_ref.dtype)


def result(grad, w_proj):
    vmem = pl.BlockSpec(memory_space=pltpu.VMEM)
    rows, depth = grad.shape[0], w_proj.shape[0]
    return pl.pallas_call(
        result_kernel,
        out_shape=jax.ShapeDtypeStruct((rows, depth), grad.dtype),
        in_specs=[vmem] * 2,
        out_specs=vmem,
        compiler_params=pltpu.CompilerParams(vmem_limit_bytes=16 * 2**20),
        cost_estimate=pl.CostEstimate(
            flops=2 * rows * w_proj.size, bytes_accessed=2 * w_proj.size, transcendentals=0
        ),
    )(grad, w_proj)


def pair_kernel(first_ref, second_ref, out_ref):
    half = first_ref.shape[0]
    out_ref[:half] = first_ref[...]
    out_ref[half:] = second_ref[...]


def side_by_side(first, second, flops):
    vmem = pl.BlockSpec(memory_space=pltpu.VMEM)
    return pl.pallas_call(
        pair_kernel,
        out_shape=jax.ShapeDtypeStruct((2 * first.shape[0], first.shape[1]), first.dtype),
        in_specs=[vmem, vmem],
        out_specs=vmem,
        compiler_params=pltpu.CompilerParams(vmem_limit_bytes=16 * 2**20),
        cost_estimate=pl.CostEstimate(flops=flops, bytes_accessed=0, transcendentals=0),
    )(first, second)


def after_kernel(value_ref, first_ref, same_ref):
    pass


def after(value, first, flops):
    anywhere = pl.BlockSpec(memory_space=pl.ANY)
    return pl.pallas_call(
        after_kernel,
        out_shape=jax.ShapeDtypeStruct(value.shape, value.dtype),
        in_specs=[anywhere, anywhere],
        out_specs=anywhere,
        input_output_aliases={0: 0},
        compiler_params=pltpu.CompilerParams(vmem_limit_bytes=16 * 2**20),
        cost_estimate=pl.CostEstimate(flops=flops, bytes_accessed=0, transcendentals=0),
    )(value, first)


def tile_kernel(count, more, last, *refs):
    f32, bf16 = jnp.float32, jnp.bfloat16
    rates_ref, col_ref = refs[:2]
    pieces, refs = refs[2 : 2 + count], refs[2 + count :]
    held, refs = (refs[:2], refs[2:]) if more else (None, refs)
    outs, rows_ref = refs[:-1], refs[-1]
    width = col_ref.shape[1] - PAD
    n_rows = rows_ref.shape[0]

    turned, filled = [], 0
    for piece in pieces:
        rows_ref[filled : filled + piece.shape[0]] = piece[:, :width]
        filled += piece.shape[0]
        turned.append(piece[:, width:].astype(f32).T)
    turned = jnp.concatenate([value[:8] for value in turned], axis=1)
    row_sign = turned[0:1]
    row_norm = turned[1:2] + turned[2:3] + turned[3:4]

    scales = [rates_ref[band] * (-LOG2E / width) for band in range(rates_ref.shape[0])]
    step = min(256, col_ref.shape[0])
    for start in range(0, col_ref.shape[0], step):
        place = slice(start, start + step)
        col_z = col_ref[place, :width]
        tail = col_ref[place, width:].astype(f32)
        col_norm = tail[:, 1:2] + tail[:, 2:3] + tail[:, 3:4]
        cross = lax.dot_general(
            col_z, rows_ref[...], (((1,), (1,)), ((), ())), preferred_element_type=f32
        )
        dist = jnp.maximum(col_norm + row_norm - 2.0 * cross, 0.0)
        kernel = jnp.zeros((step, n_rows), f32)
        for band, scale in enumerate(scales):
            kernel += rates_ref[band] * jnp.exp2(scale * dist)
        kernel *= row_sign
        total = jnp.broadcast_to(jnp.sum(kernel, axis=1, keepdims=True), (step, PAD))
        other = jnp.dot(kernel.astype(bf16), rows_ref[...], preferred_element_type=f32)
        if more:
            total += held[0][place]
            other += held[1][place]
        if last:
            factor = (-32.0 / width) * tail[:, 0:1]
            wide = col_z.astype(f32)
            outs[0][place] = (factor * (total[:, :1] * wide - other)).astype(bf16)
        else:
            outs[0][place] = total
            outs[1][place] = other


def tiles(pieces, col, rates, held=(), last=False):
    f32, bf16 = jnp.float32, jnp.bfloat16
    n_cols, width = col.shape[0], col.shape[1] - PAD
    n_rows = sum(piece.shape[0] for piece in pieces)
    vmem = pl.BlockSpec(memory_space=pltpu.VMEM)
    if last:
        out_shape = jax.ShapeDtypeStruct((n_cols, width), bf16)
    else:
        out_shape = (
            jax.ShapeDtypeStruct((n_cols, PAD), f32),
            jax.ShapeDtypeStruct((n_cols, width), f32),
        )
    pairs = n_rows * n_cols
    return pl.pallas_call(
        functools.partial(tile_kernel, len(pieces), bool(held), last),
        out_shape=out_shape,
        in_specs=[pl.BlockSpec(memory_space=pltpu.SMEM)] + [vmem] * (1 + len(pieces) + len(held)),
        out_specs=vmem if last else (vmem, vmem),
        scratch_shapes=[pltpu.VMEM((n_rows, width), bf16)],
        compiler_params=pltpu.CompilerParams(vmem_limit_bytes=32 * 2**20),
        cost_estimate=pl.CostEstimate(
            flops=4 * pairs * width, bytes_accessed=4 * n_cols * width, transcendentals=5 * pairs
        ),
    )(rates, col, *pieces, *held)


def shards(features, w_proj, flags, rates):
    f32, bf16 = jnp.float32, jnp.bfloat16
    group = features.shape[0]
    width = w_proj.shape[1]
    n_row = lax.axis_size("row")
    n_col = lax.axis_size("col")
    half, quarter = group // 2, group // 4
    tpos = lax.axis_index("tensor")
    high, core = tpos // 2 == 1, tpos % 2 == 1

    def move(value, shift):
        return lax.ppermute(value, ZLINE, line_permutation(shift, n_row))

    def other_core(value):
        return move(value, lambda chip, core: (chip, 1 - core))

    away, kept = projection(jnp.reshape(tpos % 2, (1,)), features, w_proj)
    partial = (kept + other_core(away).astype(f32)).astype(bf16)
    far = move(partial, lambda chip, core: (chip + n_row, core))
    signs = (1 - 2 * flags).astype(f32)
    s_half = pick(core, signs[:half], signs[half:])
    block = whole_block(partial, far, jnp.broadcast_to(s_half[:, None], (half, PAD)))

    far_block = move(block, lambda chip, core: (chip + (n_row // 2) * (1 - 2 * core), core))
    pair = side_by_side(block, far_block, FLOPS)
    two_away = move(pair, lambda chip, core: (chip + 2 - 4 * core, core))
    other_pair = other_core(pair)
    one_away = move(
        side_by_side(pair, other_pair, 0), lambda chip, core: (chip + 1 - 2 * core, core)
    )
    own = pick(high, block[:quarter], block[quarter:])
    col = lax.all_to_all(
        jnp.broadcast_to(own[None], (n_col,) + own.shape), "col", 0, 0, tiled=True
    ).reshape(n_col * quarter, width + PAD)
    sums = tiles([pair, other_pair], col, rates)
    other_two_away = after(other_core(two_away), sums[0], FLOPS // 20)
    one_away = after(one_away, other_two_away, 0)
    sums = tiles([two_away, other_two_away], col, rates, sums, False)
    part = tiles([one_away, other_core(one_away)], col, rates, sums, True)
    parts = lax.all_to_all(part.reshape(n_col, quarter, width), "col", 0, 0, tiled=True)
    grad = jnp.sum(parts.astype(f32), axis=0).astype(bf16)
    grad_far = move(grad, lambda chip, core: (chip + n_row, core))
    grad = pick(
        high, jnp.concatenate([grad, grad_far], axis=0), jnp.concatenate([grad_far, grad], axis=0)
    )
    grad_other = other_core(grad)
    grad = pick(
        core,
        jnp.concatenate([grad, grad_other], axis=0),
        jnp.concatenate([grad_other, grad], axis=0),
    )
    return result(grad, w_proj)


def solution(mesh):
    in_specs = (P(("row", "col"), "tensor"), P("tensor", None), P(("row", "col")), P())
    out_specs = P(("row", "col"), "tensor")
    return jax.shard_map(shards, mesh=mesh, in_specs=in_specs, out_specs=out_specs, check_vma=False)
```

```python
import functools
import math

import jax
import jax.numpy as jnp
from jax import lax
from jax.experimental import pallas as pl
from jax.experimental.pallas import tpu as pltpu
from jax.sharding import PartitionSpec as P

ZLINE = ("tensor", "row")
PAD = 128
LOG2E = math.log2(math.e)
FLOPS = 4 * 10**10


def line_permutation(shift, n_row):
    length = 2 * n_row
    pairs = []
    for chip in range(length):
        for core in range(2):
            chip2, core2 = shift(chip, core)
            chip2 %= length
            source = ((chip // n_row) * 2 + core) * n_row + chip % n_row
            target = ((chip2 // n_row) * 2 + core2) * n_row + chip2 % n_row
            pairs.append((source, target))
    return pairs


def pick(second, low, high):
    return jnp.where(second, high, low)

CHUNKS = 4


def projection_kernel(core_ref, features_ref, w_ref, away_ref, kept_ref, rows, weights, total, sem):
    copies = []
    depth = rows.shape[1] // CHUNKS
    for index in range(CHUNKS):
        place = pl.ds(index * depth, depth)
        copies.append(
            (
                pltpu.make_async_copy(features_ref.at[:, place], rows.at[:, place], sem.at[0, index]),
                pltpu.make_async_copy(w_ref.at[place], weights.at[place], sem.at[1, index]),
            )
        )
        for copy in copies[-1]:
            copy.start()
    value = None
    for index in range(CHUNKS):
        place = slice(index * depth, (index + 1) * depth)
        for copy in copies[index]:
            copy.wait()
        term = jnp.dot(rows[:, place], weights[place], preferred_element_type=jnp.float32)
        value = term if value is None else value + term
    total[...] = value
    half = kept_ref.shape[0]
    core = core_ref[0]
    away = total[pl.ds(pl.multiple_of((1 - core) * half, half), half)]
    away_ref[...] = away.astype(away_ref.dtype)
    kept_ref[...] = total[pl.ds(pl.multiple_of(core * half, half), half)]


def projection(core, features, w_proj):
    rows, width = features.shape[0], w_proj.shape[1]
    vmem, anywhere = pl.BlockSpec(memory_space=pltpu.VMEM), pl.BlockSpec(memory_space=pl.ANY)
    return pl.pallas_call(
        projection_kernel,
        out_shape=(
            jax.ShapeDtypeStruct((rows // 2, width), jnp.bfloat16),
            jax.ShapeDtypeStruct((rows // 2, width), jnp.float32),
        ),
        in_specs=[pl.BlockSpec(memory_space=pltpu.SMEM), anywhere, anywhere],
        out_specs=(vmem, vmem),
        scratch_shapes=[
            pltpu.VMEM(features.shape, features.dtype),
            pltpu.VMEM(w_proj.shape, w_proj.dtype),
            pltpu.VMEM((rows, width), jnp.float32),
            pltpu.SemaphoreType.DMA((2, CHUNKS)),
        ],
        compiler_params=pltpu.CompilerParams(vmem_limit_bytes=60 * 2**20),
        cost_estimate=pl.CostEstimate(
            flops=2 * rows * width * w_proj.shape[0],
            bytes_accessed=2 * w_proj.shape[0] * width,
            transcendentals=0,
        ),
    )(core, features, w_proj)


def block_kernel(near_ref, far_ref, block_ref):
    f32, bf16 = jnp.float32, jnp.bfloat16
    half, width = far_ref.shape
    rows = (near_ref[:, :width].astype(f32) + far_ref[...].astype(f32)).astype(bf16)
    block_ref[:, :width] = rows
    norm = jnp.sum(jnp.square(rows.astype(f32)), axis=1, keepdims=True)
    first = norm.astype(bf16).astype(f32)
    second = (norm - first).astype(bf16).astype(f32)
    third = norm - first - second
    lane = lax.broadcasted_iota(jnp.int32, (half, PAD), 1)
    tail = jnp.where(lane == 1, first, jnp.where(lane == 2, second, third))
    block_ref[:, width:] = jnp.where(lane == 0, near_ref[:, width:].astype(f32), tail).astype(bf16)


def whole_block(near, far):
    vmem = pl.BlockSpec(memory_space=pltpu.VMEM)
    half, width = far.shape
    return pl.pallas_call(
        block_kernel,
        out_shape=jax.ShapeDtypeStruct((half, width + PAD), near.dtype),
        in_specs=[vmem] * 2,
        out_specs=vmem,
        compiler_params=pltpu.CompilerParams(vmem_limit_bytes=16 * 2**20),
        cost_estimate=pl.CostEstimate(
            flops=4 * half * width, bytes_accessed=6 * half * width, transcendentals=0
        ),
    )(near, far)


def result_kernel(grad_ref, w_ref, out_ref):
    out_ref[...] = lax.dot_general(
        grad_ref[...], w_ref[...], (((1,), (1,)), ((), ())), preferred_element_type=jnp.float32
    ).astype(out_ref.dtype)


def result(grad, w_proj):
    vmem = pl.BlockSpec(memory_space=pltpu.VMEM)
    rows, depth = grad.shape[0], w_proj.shape[0]
    return pl.pallas_call(
        result_kernel,
        out_shape=jax.ShapeDtypeStruct((rows, depth), grad.dtype),
        in_specs=[vmem] * 2,
        out_specs=vmem,
        compiler_params=pltpu.CompilerParams(vmem_limit_bytes=16 * 2**20),
        cost_estimate=pl.CostEstimate(
            flops=2 * rows * w_proj.size, bytes_accessed=2 * w_proj.size, transcendentals=0
        ),
    )(grad, w_proj)


def pair_kernel(first_ref, second_ref, out_ref):
    half = first_ref.shape[0]
    out_ref[:half] = first_ref[...]
    out_ref[half:] = second_ref[...]


def side_by_side(first, second, flops):
    vmem = pl.BlockSpec(memory_space=pltpu.VMEM)
    return pl.pallas_call(
        pair_kernel,
        out_shape=jax.ShapeDtypeStruct((2 * first.shape[0], first.shape[1]), first.dtype),
        in_specs=[vmem, vmem],
        out_specs=vmem,
        compiler_params=pltpu.CompilerParams(vmem_limit_bytes=16 * 2**20),
        cost_estimate=pl.CostEstimate(flops=flops, bytes_accessed=0, transcendentals=0),
    )(first, second)


def after_kernel(value_ref, first_ref, same_ref):
    pass


def after(value, first, flops):
    anywhere = pl.BlockSpec(memory_space=pl.ANY)
    return pl.pallas_call(
        after_kernel,
        out_shape=jax.ShapeDtypeStruct(value.shape, value.dtype),
        in_specs=[anywhere, anywhere],
        out_specs=anywhere,
        input_output_aliases={0: 0},
        compiler_params=pltpu.CompilerParams(vmem_limit_bytes=16 * 2**20),
        cost_estimate=pl.CostEstimate(flops=flops, bytes_accessed=0, transcendentals=0),
    )(value, first)


def tile_kernel(count, more, last, *refs):
    f32, bf16 = jnp.float32, jnp.bfloat16
    rates_ref, col_ref = refs[:2]
    pieces, refs = refs[2 : 2 + count], refs[2 + count :]
    held, refs = (refs[:2], refs[2:]) if more else (None, refs)
    outs, rows_ref = refs[:-1], refs[-1]
    width = col_ref.shape[1] - PAD
    n_rows = rows_ref.shape[0]

    turned, filled = [], 0
    for piece in pieces:
        rows_ref[filled : filled + piece.shape[0]] = piece[:, :width]
        filled += piece.shape[0]
        turned.append(piece[:, width:].astype(f32).T)
    turned = jnp.concatenate([value[:8] for value in turned], axis=1)
    row_sign = turned[0:1]
    row_norm = turned[1:2] + turned[2:3] + turned[3:4]

    scales = [rates_ref[band] * (-LOG2E / width) for band in range(rates_ref.shape[0])]
    step = min(256, col_ref.shape[0])
    for start in range(0, col_ref.shape[0], step):
        place = slice(start, start + step)
        col_z = col_ref[place, :width]
        tail = col_ref[place, width:].astype(f32)
        col_norm = tail[:, 1:2] + tail[:, 2:3] + tail[:, 3:4]
        cross = lax.dot_general(
            col_z, rows_ref[...], (((1,), (1,)), ((), ())), preferred_element_type=f32
        )
        dist = jnp.maximum(col_norm + row_norm - 2.0 * cross, 0.0)
        kernel = jnp.zeros((step, n_rows), f32)
        for band, scale in enumerate(scales):
            kernel += rates_ref[band] * jnp.exp2(scale * dist)
        kernel *= row_sign
        total = jnp.broadcast_to(jnp.sum(kernel, axis=1, keepdims=True), (step, PAD))
        other = jnp.dot(kernel.astype(bf16), rows_ref[...], preferred_element_type=f32)
        if more:
            total += held[0][place]
            other += held[1][place]
        if last:
            factor = (-32.0 / width) * tail[:, 0:1]
            wide = col_z.astype(f32)
            outs[0][place] = (factor * (total[:, :1] * wide - other)).astype(bf16)
        else:
            outs[0][place] = total
            outs[1][place] = other


def tiles(pieces, col, rates, held=(), last=False):
    f32, bf16 = jnp.float32, jnp.bfloat16
    n_cols, width = col.shape[0], col.shape[1] - PAD
    n_rows = sum(piece.shape[0] for piece in pieces)
    vmem = pl.BlockSpec(memory_space=pltpu.VMEM)
    if last:
        out_shape = jax.ShapeDtypeStruct((n_cols, width), bf16)
    else:
        out_shape = (
            jax.ShapeDtypeStruct((n_cols, PAD), f32),
            jax.ShapeDtypeStruct((n_cols, width), f32),
        )
    pairs = n_rows * n_cols
    return pl.pallas_call(
        functools.partial(tile_kernel, len(pieces), bool(held), last),
        out_shape=out_shape,
        in_specs=[pl.BlockSpec(memory_space=pltpu.SMEM)] + [vmem] * (1 + len(pieces) + len(held)),
        out_specs=vmem if last else (vmem, vmem),
        scratch_shapes=[pltpu.VMEM((n_rows, width), bf16)],
        compiler_params=pltpu.CompilerParams(vmem_limit_bytes=32 * 2**20),
        cost_estimate=pl.CostEstimate(
            flops=4 * pairs * width, bytes_accessed=4 * n_cols * width, transcendentals=5 * pairs
        ),
    )(rates, col, *pieces, *held)


def shards(features, w_proj, flags, rates):
    f32, bf16 = jnp.float32, jnp.bfloat16
    group = features.shape[0]
    width = w_proj.shape[1]
    n_row = lax.axis_size("row")
    n_col = lax.axis_size("col")
    half, quarter = group // 2, group // 4
    tpos = lax.axis_index("tensor")
    high, core = tpos // 2 == 1, tpos % 2 == 1

    def move(value, shift):
        return lax.ppermute(value, ZLINE, line_permutation(shift, n_row))

    def other_core(value):
        return move(value, lambda chip, core: (chip, 1 - core))

    away, kept = projection(jnp.reshape(tpos % 2, (1,)), features, w_proj)
    partial = (kept + other_core(away).astype(f32)).astype(bf16)
    signs = (1 - 2 * flags).astype(bf16)
    s_half = pick(core, signs[:half], signs[half:])
    signed = jnp.concatenate([partial, jnp.broadcast_to(s_half[:, None], (half, PAD))], axis=1)

    step = n_row // 2
    block = whole_block(
        move(signed, lambda chip, core: (chip + step, core)),
        move(partial, lambda chip, core: (chip - step, core)),
    )

    far_block = move(block, lambda chip, core: (chip + step * (1 - 2 * core), core))
    pair = side_by_side(block, far_block, FLOPS)
    two_away = move(pair, lambda chip, core: (chip + 2 - 4 * core, core))
    other_pair = other_core(pair)
    one_away = move(
        side_by_side(pair, other_pair, 0), lambda chip, core: (chip + 1 - 2 * core, core)
    )
    own = pick(high, block[:quarter], block[quarter:])
    col = lax.all_to_all(
        jnp.broadcast_to(own[None], (n_col,) + own.shape), "col", 0, 0, tiled=True
    ).reshape(n_col * quarter, width + PAD)
    sums = tiles([pair, other_pair], col, rates)
    other_two_away = after(other_core(two_away), sums[0], FLOPS // 20)
    one_away = after(one_away, other_two_away, 0)
    sums = tiles([two_away, other_two_away], col, rates, sums, False)
    part = tiles([one_away, other_core(one_away)], col, rates, sums, True)
    parts = lax.all_to_all(part.reshape(n_col, quarter, width), "col", 0, 0, tiled=True)
    grad = jnp.sum(parts.astype(f32), axis=0).astype(bf16)
    above = move(grad, lambda chip, core: (chip - step, core))
    below = move(grad, lambda chip, core: (chip + step, core))
    grad = pick(
        high ^ (lax.axis_index("row") >= step),
        jnp.concatenate([above, below], axis=0),
        jnp.concatenate([below, above], axis=0),
    )
    grad_other = other_core(grad)
    grad = pick(
        core,
        jnp.concatenate([grad, grad_other], axis=0),
        jnp.concatenate([grad_other, grad], axis=0),
    )
    return result(grad, w_proj)


def solution(mesh):
    in_specs = (P(("row", "col"), "tensor"), P("tensor", None), P(("row", "col")), P())
    out_specs = P(("row", "col"), "tensor")
    return jax.shard_map(shards, mesh=mesh, in_specs=in_specs, out_specs=out_specs, check_vma=False)
```

```python
import functools
import math

import jax
import jax.numpy as jnp
from jax import lax
from jax.experimental import pallas as pl
from jax.experimental.pallas import tpu as pltpu
from jax.sharding import PartitionSpec as P

ZLINE = ("tensor", "row")
PAD = 128
LOG2E = math.log2(math.e)
FLOPS = 4 * 10**10


def line_permutation(shift, n_row):
    length = 2 * n_row
    pairs = []
    for chip in range(length):
        for core in range(2):
            chip2, core2 = shift(chip, core)
            chip2 %= length
            source = ((chip // n_row) * 2 + core) * n_row + chip % n_row
            target = ((chip2 // n_row) * 2 + core2) * n_row + chip2 % n_row
            pairs.append((source, target))
    return pairs


def pick(second, low, high):
    return jnp.where(second, high, low)

CHUNKS = 4


def projection_kernel(core_ref, features_ref, w_ref, away_ref, kept_ref, rows, weights, total, sem):
    copies = []
    depth = rows.shape[1] // CHUNKS
    for index in range(CHUNKS):
        place = pl.ds(index * depth, depth)
        copies.append(
            (
                pltpu.make_async_copy(features_ref.at[:, place], rows.at[:, place], sem.at[0, index]),
                pltpu.make_async_copy(w_ref.at[place], weights.at[place], sem.at[1, index]),
            )
        )
        for copy in copies[-1]:
            copy.start()
    value = None
    for index in range(CHUNKS):
        place = slice(index * depth, (index + 1) * depth)
        for copy in copies[index]:
            copy.wait()
        term = jnp.dot(rows[:, place], weights[place], preferred_element_type=jnp.float32)
        value = term if value is None else value + term
    total[...] = value
    half = kept_ref.shape[0]
    core = core_ref[0]
    away = total[pl.ds(pl.multiple_of((1 - core) * half, half), half)]
    away_ref[...] = away.astype(away_ref.dtype)
    kept_ref[...] = total[pl.ds(pl.multiple_of(core * half, half), half)]


def projection(core, features, w_proj):
    rows, width = features.shape[0], w_proj.shape[1]
    vmem, anywhere = pl.BlockSpec(memory_space=pltpu.VMEM), pl.BlockSpec(memory_space=pl.ANY)
    return pl.pallas_call(
        projection_kernel,
        out_shape=(
            jax.ShapeDtypeStruct((rows // 2, width), jnp.bfloat16),
            jax.ShapeDtypeStruct((rows // 2, width), jnp.float32),
        ),
        in_specs=[pl.BlockSpec(memory_space=pltpu.SMEM), anywhere, anywhere],
        out_specs=(vmem, vmem),
        scratch_shapes=[
            pltpu.VMEM(features.shape, features.dtype),
            pltpu.VMEM(w_proj.shape, w_proj.dtype),
            pltpu.VMEM((rows, width), jnp.float32),
            pltpu.SemaphoreType.DMA((2, CHUNKS)),
        ],
        compiler_params=pltpu.CompilerParams(vmem_limit_bytes=60 * 2**20),
        cost_estimate=pl.CostEstimate(
            flops=2 * rows * width * w_proj.shape[0],
            bytes_accessed=2 * w_proj.shape[0] * width,
            transcendentals=0,
        ),
    )(core, features, w_proj)


def block_kernel(near_ref, far_ref, signs_ref, block_ref):
    f32, bf16 = jnp.float32, jnp.bfloat16
    half, width = near_ref.shape
    rows = (near_ref[...].astype(f32) + far_ref[...].astype(f32)).astype(bf16)
    block_ref[:, :width] = rows
    norm = jnp.sum(jnp.square(rows.astype(f32)), axis=1, keepdims=True)
    first = norm.astype(bf16).astype(f32)
    second = (norm - first).astype(bf16).astype(f32)
    third = norm - first - second
    lane = lax.broadcasted_iota(jnp.int32, (half, PAD), 1)
    tail = jnp.where(lane == 1, first, jnp.where(lane == 2, second, third))
    block_ref[:, width:] = jnp.where(lane == 0, signs_ref[...], tail).astype(bf16)


def whole_block(near, far, signs):
    vmem = pl.BlockSpec(memory_space=pltpu.VMEM)
    half, width = near.shape
    return pl.pallas_call(
        block_kernel,
        out_shape=jax.ShapeDtypeStruct((half, width + PAD), near.dtype),
        in_specs=[vmem] * 3,
        out_specs=vmem,
        compiler_params=pltpu.CompilerParams(vmem_limit_bytes=16 * 2**20),
        cost_estimate=pl.CostEstimate(
            flops=4 * half * width, bytes_accessed=6 * half * width, transcendentals=0
        ),
    )(near, far, signs)


def result_kernel(grad_ref, w_ref, out_ref):
    out_ref[...] = lax.dot_general(
        grad_ref[...], w_ref[...], (((1,), (1,)), ((), ())), preferred_element_type=jnp.float32
    ).astype(out_ref.dtype)


def result(grad, w_proj):
    vmem = pl.BlockSpec(memory_space=pltpu.VMEM)
    rows, depth = grad.shape[0], w_proj.shape[0]
    return pl.pallas_call(
        result_kernel,
        out_shape=jax.ShapeDtypeStruct((rows, depth), grad.dtype),
        in_specs=[vmem] * 2,
        out_specs=vmem,
        compiler_params=pltpu.CompilerParams(vmem_limit_bytes=16 * 2**20),
        cost_estimate=pl.CostEstimate(
            flops=2 * rows * w_proj.size, bytes_accessed=2 * w_proj.size, transcendentals=0
        ),
    )(grad, w_proj)


def sum_kernel(parts_ref, out_ref):
    total = parts_ref[0].astype(jnp.float32)
    for index in range(1, parts_ref.shape[0]):
        total += parts_ref[index].astype(jnp.float32)
    out_ref[...] = total.astype(out_ref.dtype)


def summed(parts):
    vmem = pl.BlockSpec(memory_space=pltpu.VMEM)
    return pl.pallas_call(
        sum_kernel,
        out_shape=jax.ShapeDtypeStruct(parts.shape[1:], parts.dtype),
        in_specs=[vmem],
        out_specs=vmem,
        compiler_params=pltpu.CompilerParams(vmem_limit_bytes=16 * 2**20),
        cost_estimate=pl.CostEstimate(
            flops=parts.size, bytes_accessed=2 * parts.size, transcendentals=0
        ),
    )(parts)


def pair_kernel(first_ref, second_ref, out_ref):
    half = first_ref.shape[0]
    out_ref[:half] = first_ref[...]
    out_ref[half:] = second_ref[...]


def side_by_side(first, second, flops):
    vmem = pl.BlockSpec(memory_space=pltpu.VMEM)
    return pl.pallas_call(
        pair_kernel,
        out_shape=jax.ShapeDtypeStruct((2 * first.shape[0], first.shape[1]), first.dtype),
        in_specs=[vmem, vmem],
        out_specs=vmem,
        compiler_params=pltpu.CompilerParams(vmem_limit_bytes=16 * 2**20),
        cost_estimate=pl.CostEstimate(flops=flops, bytes_accessed=0, transcendentals=0),
    )(first, second)


def after_kernel(value_ref, first_ref, same_ref):
    pass


def after(value, first, flops):
    anywhere = pl.BlockSpec(memory_space=pl.ANY)
    return pl.pallas_call(
        after_kernel,
        out_shape=jax.ShapeDtypeStruct(value.shape, value.dtype),
        in_specs=[anywhere, anywhere],
        out_specs=anywhere,
        input_output_aliases={0: 0},
        compiler_params=pltpu.CompilerParams(vmem_limit_bytes=16 * 2**20),
        cost_estimate=pl.CostEstimate(flops=flops, bytes_accessed=0, transcendentals=0),
    )(value, first)


def tile_kernel(count, more, last, *refs):
    f32, bf16 = jnp.float32, jnp.bfloat16
    rates_ref, col_ref = refs[:2]
    pieces, refs = refs[2 : 2 + count], refs[2 + count :]
    held, refs = (refs[:2], refs[2:]) if more else (None, refs)
    outs, rows_ref = refs[:-1], refs[-1]
    width = col_ref.shape[1] - PAD
    n_rows = rows_ref.shape[0]

    turned, filled = [], 0
    for piece in pieces:
        rows_ref[filled : filled + piece.shape[0]] = piece[:, :width]
        filled += piece.shape[0]
        turned.append(piece[:, width:].astype(f32).T)
    turned = jnp.concatenate([value[:8] for value in turned], axis=1)
    row_sign = turned[0:1]
    row_norm = turned[1:2] + turned[2:3] + turned[3:4]

    scales = [rates_ref[band] * (-LOG2E / width) for band in range(rates_ref.shape[0])]
    step = min(256, col_ref.shape[0])
    for start in range(0, col_ref.shape[0], step):
        place = slice(start, start + step)
        col_z = col_ref[place, :width]
        tail = col_ref[place, width:].astype(f32)
        col_norm = tail[:, 1:2] + tail[:, 2:3] + tail[:, 3:4]
        cross = lax.dot_general(
            col_z, rows_ref[...], (((1,), (1,)), ((), ())), preferred_element_type=f32
        )
        dist = jnp.maximum(col_norm + row_norm - 2.0 * cross, 0.0)
        kernel = jnp.zeros((step, n_rows), f32)
        for band, scale in enumerate(scales):
            kernel += rates_ref[band] * jnp.exp2(scale * dist)
        kernel *= row_sign
        total = jnp.broadcast_to(jnp.sum(kernel, axis=1, keepdims=True), (step, PAD))
        other = jnp.dot(kernel.astype(bf16), rows_ref[...], preferred_element_type=f32)
        if more:
            total += held[0][place]
            other += held[1][place]
        if last:
            factor = (-32.0 / width) * tail[:, 0:1]
            wide = col_z.astype(f32)
            outs[0][place] = (factor * (total[:, :1] * wide - other)).astype(bf16)
        else:
            outs[0][place] = total
            outs[1][place] = other


def tiles(pieces, col, rates, held=(), last=False):
    f32, bf16 = jnp.float32, jnp.bfloat16
    n_cols, width = col.shape[0], col.shape[1] - PAD
    n_rows = sum(piece.shape[0] for piece in pieces)
    vmem = pl.BlockSpec(memory_space=pltpu.VMEM)
    if last:
        out_shape = jax.ShapeDtypeStruct((n_cols, width), bf16)
    else:
        out_shape = (
            jax.ShapeDtypeStruct((n_cols, PAD), f32),
            jax.ShapeDtypeStruct((n_cols, width), f32),
        )
    pairs = n_rows * n_cols
    return pl.pallas_call(
        functools.partial(tile_kernel, len(pieces), bool(held), last),
        out_shape=out_shape,
        in_specs=[pl.BlockSpec(memory_space=pltpu.SMEM)] + [vmem] * (1 + len(pieces) + len(held)),
        out_specs=vmem if last else (vmem, vmem),
        scratch_shapes=[pltpu.VMEM((n_rows, width), bf16)],
        compiler_params=pltpu.CompilerParams(vmem_limit_bytes=32 * 2**20),
        cost_estimate=pl.CostEstimate(
            flops=4 * pairs * width, bytes_accessed=4 * n_cols * width, transcendentals=5 * pairs
        ),
    )(rates, col, *pieces, *held)


def shards(features, w_proj, flags, rates):
    f32, bf16 = jnp.float32, jnp.bfloat16
    group = features.shape[0]
    width = w_proj.shape[1]
    n_row = lax.axis_size("row")
    n_col = lax.axis_size("col")
    half, quarter = group // 2, group // 4
    tpos = lax.axis_index("tensor")
    high, core = tpos // 2 == 1, tpos % 2 == 1

    def move(value, shift):
        return lax.ppermute(value, ZLINE, line_permutation(shift, n_row))

    def other_core(value):
        return move(value, lambda chip, core: (chip, 1 - core))

    away, kept = projection(jnp.reshape(tpos % 2, (1,)), features, w_proj)
    partial = (kept + other_core(away).astype(f32)).astype(bf16)
    far = move(partial, lambda chip, core: (chip + n_row, core))
    signs = (1 - 2 * flags).astype(f32)
    s_half = pick(core, signs[:half], signs[half:])
    block = whole_block(partial, far, jnp.broadcast_to(s_half[:, None], (half, PAD)))

    far_block = move(block, lambda chip, core: (chip + (n_row // 2) * (1 - 2 * core), core))
    pair = side_by_side(block, far_block, FLOPS)
    other_pair = other_core(pair)
    two_away = move(pair, lambda chip, core: (chip + 2 - 4 * core, core))
    next_own = move(pair, lambda chip, core: (chip + 1 - 2 * core, core))
    next_other = move(other_pair, lambda chip, core: (chip + 1 - 2 * core, core))
    own = pick(high, block[:quarter], block[quarter:])
    col = lax.all_to_all(
        jnp.broadcast_to(own[None], (n_col,) + own.shape), "col", 0, 0, tiled=True
    ).reshape(n_col * quarter, width + PAD)
    sums = tiles([pair, other_pair], col, rates)
    two_away = after(two_away, sums[0], 0)
    next_own = after(next_own, sums[0], 0)
    middle = [two_away, other_core(two_away), next_own, other_core(next_own)]
    sums = tiles(middle, col, rates, sums, False)
    next_other = after(next_other, middle[1], 0)
    part = tiles([next_other, other_core(next_other)], col, rates, sums, True)
    parts = lax.all_to_all(part.reshape(n_col, quarter, width), "col", 0, 0, tiled=True)
    grad = summed(parts)
    grad_far = move(grad, lambda chip, core: (chip + n_row, core))
    grad = pick(
        high, jnp.concatenate([grad, grad_far], axis=0), jnp.concatenate([grad_far, grad], axis=0)
    )
    grad_other = other_core(grad)
    grad = pick(
        core,
        jnp.concatenate([grad, grad_other], axis=0),
        jnp.concatenate([grad_other, grad], axis=0),
    )
    return result(grad, w_proj)


def solution(mesh):
    in_specs = (P(("row", "col"), "tensor"), P("tensor", None), P(("row", "col")), P())
    out_specs = P(("row", "col"), "tensor")
    return jax.shard_map(shards, mesh=mesh, in_specs=in_specs, out_specs=out_specs, check_vma=False)
```

```python
import functools
import math

import jax
import jax.numpy as jnp
from jax import lax
from jax.experimental import pallas as pl
from jax.experimental.pallas import tpu as pltpu
from jax.sharding import PartitionSpec as P

ZLINE = ("tensor", "row")
PAD = 128
LOG2E = math.log2(math.e)
FLOPS = 4 * 10**10


def line_permutation(shift, n_row):
    length = 2 * n_row
    pairs = []
    for chip in range(length):
        for core in range(2):
            chip2, core2 = shift(chip, core)
            chip2 %= length
            source = ((chip // n_row) * 2 + core) * n_row + chip % n_row
            target = ((chip2 // n_row) * 2 + core2) * n_row + chip2 % n_row
            pairs.append((source, target))
    return pairs


def pick(second, low, high):
    return jnp.where(second, high, low)

CHUNKS = 4


def projection_kernel(core_ref, features_ref, w_ref, away_ref, kept_ref, rows, weights, total, sem):
    copies = []
    depth = rows.shape[1] // CHUNKS
    for index in range(CHUNKS):
        place = pl.ds(index * depth, depth)
        copies.append(
            (
                pltpu.make_async_copy(features_ref.at[:, place], rows.at[:, place], sem.at[0, index]),
                pltpu.make_async_copy(w_ref.at[place], weights.at[place], sem.at[1, index]),
            )
        )
        for copy in copies[-1]:
            copy.start()
    value = None
    for index in range(CHUNKS):
        place = slice(index * depth, (index + 1) * depth)
        for copy in copies[index]:
            copy.wait()
        term = jnp.dot(rows[:, place], weights[place], preferred_element_type=jnp.float32)
        value = term if value is None else value + term
    total[...] = value
    quarter = kept_ref.shape[0] // 2
    core = core_ref[0]
    for index in range(2):
        place = slice(index * quarter, (index + 1) * quarter)
        start = pl.multiple_of((2 * index + 1 - core) * quarter, quarter)
        away_ref[place] = total[pl.ds(start, quarter)].astype(away_ref.dtype)
        start = pl.multiple_of((2 * index + core) * quarter, quarter)
        kept_ref[place] = total[pl.ds(start, quarter)]


def projection(core, features, w_proj):
    rows, width = features.shape[0], w_proj.shape[1]
    vmem, anywhere = pl.BlockSpec(memory_space=pltpu.VMEM), pl.BlockSpec(memory_space=pl.ANY)
    return pl.pallas_call(
        projection_kernel,
        out_shape=(
            jax.ShapeDtypeStruct((rows // 2, width), jnp.bfloat16),
            jax.ShapeDtypeStruct((rows // 2, width), jnp.float32),
        ),
        in_specs=[pl.BlockSpec(memory_space=pltpu.SMEM), anywhere, anywhere],
        out_specs=(vmem, vmem),
        scratch_shapes=[
            pltpu.VMEM(features.shape, features.dtype),
            pltpu.VMEM(w_proj.shape, w_proj.dtype),
            pltpu.VMEM((rows, width), jnp.float32),
            pltpu.SemaphoreType.DMA((2, CHUNKS)),
        ],
        compiler_params=pltpu.CompilerParams(vmem_limit_bytes=60 * 2**20),
        cost_estimate=pl.CostEstimate(
            flops=2 * rows * width * w_proj.shape[0],
            bytes_accessed=2 * w_proj.shape[0] * width,
            transcendentals=0,
        ),
    )(core, features, w_proj)


def block_kernel(near_ref, far_ref, signs_ref, block_ref):
    f32, bf16 = jnp.float32, jnp.bfloat16
    half, width = near_ref.shape
    rows = (near_ref[...].astype(f32) + far_ref[...].astype(f32)).astype(bf16)
    block_ref[:, :width] = rows
    norm = jnp.sum(jnp.square(rows.astype(f32)), axis=1, keepdims=True)
    first = norm.astype(bf16).astype(f32)
    second = (norm - first).astype(bf16).astype(f32)
    third = norm - first - second
    lane = lax.broadcasted_iota(jnp.int32, (half, PAD), 1)
    tail = jnp.where(lane == 1, first, jnp.where(lane == 2, second, third))
    block_ref[:, width:] = jnp.where(lane == 0, signs_ref[...], tail).astype(bf16)


def whole_block(near, far, signs):
    vmem = pl.BlockSpec(memory_space=pltpu.VMEM)
    half, width = near.shape
    return pl.pallas_call(
        block_kernel,
        out_shape=jax.ShapeDtypeStruct((half, width + PAD), near.dtype),
        in_specs=[vmem] * 3,
        out_specs=vmem,
        compiler_params=pltpu.CompilerParams(vmem_limit_bytes=16 * 2**20),
        cost_estimate=pl.CostEstimate(
            flops=4 * half * width, bytes_accessed=6 * half * width, transcendentals=0
        ),
    )(near, far, signs)


def result_kernel(grad_ref, w_ref, out_ref):
    out_ref[...] = lax.dot_general(
        grad_ref[...], w_ref[...], (((1,), (1,)), ((), ())), preferred_element_type=jnp.float32
    ).astype(out_ref.dtype)


def result(grad, w_proj):
    vmem = pl.BlockSpec(memory_space=pltpu.VMEM)
    rows, depth = grad.shape[0], w_proj.shape[0]
    return pl.pallas_call(
        result_kernel,
        out_shape=jax.ShapeDtypeStruct((rows, depth), grad.dtype),
        in_specs=[vmem] * 2,
        out_specs=vmem,
        compiler_params=pltpu.CompilerParams(vmem_limit_bytes=16 * 2**20),
        cost_estimate=pl.CostEstimate(
            flops=2 * rows * w_proj.size, bytes_accessed=2 * w_proj.size, transcendentals=0
        ),
    )(grad, w_proj)


def sum_kernel(parts_ref, out_ref):
    total = parts_ref[0].astype(jnp.float32)
    for index in range(1, parts_ref.shape[0]):
        total += parts_ref[index].astype(jnp.float32)
    out_ref[...] = total.astype(out_ref.dtype)


def summed(parts):
    vmem = pl.BlockSpec(memory_space=pltpu.VMEM)
    return pl.pallas_call(
        sum_kernel,
        out_shape=jax.ShapeDtypeStruct(parts.shape[1:], parts.dtype),
        in_specs=[vmem],
        out_specs=vmem,
        compiler_params=pltpu.CompilerParams(vmem_limit_bytes=16 * 2**20),
        cost_estimate=pl.CostEstimate(
            flops=parts.size, bytes_accessed=2 * parts.size, transcendentals=0
        ),
    )(parts)


def pair_kernel(first_ref, second_ref, out_ref):
    half = first_ref.shape[0]
    out_ref[:half] = first_ref[...]
    out_ref[half:] = second_ref[...]


def side_by_side(first, second, flops):
    vmem = pl.BlockSpec(memory_space=pltpu.VMEM)
    return pl.pallas_call(
        pair_kernel,
        out_shape=jax.ShapeDtypeStruct((2 * first.shape[0], first.shape[1]), first.dtype),
        in_specs=[vmem, vmem],
        out_specs=vmem,
        compiler_params=pltpu.CompilerParams(vmem_limit_bytes=16 * 2**20),
        cost_estimate=pl.CostEstimate(flops=flops, bytes_accessed=0, transcendentals=0),
    )(first, second)


def after_kernel(value_ref, first_ref, same_ref):
    pass


def after(value, first, flops):
    anywhere = pl.BlockSpec(memory_space=pl.ANY)
    return pl.pallas_call(
        after_kernel,
        out_shape=jax.ShapeDtypeStruct(value.shape, value.dtype),
        in_specs=[anywhere, anywhere],
        out_specs=anywhere,
        input_output_aliases={0: 0},
        compiler_params=pltpu.CompilerParams(vmem_limit_bytes=16 * 2**20),
        cost_estimate=pl.CostEstimate(flops=flops, bytes_accessed=0, transcendentals=0),
    )(value, first)


def tile_kernel(count, more, last, *refs):
    f32, bf16 = jnp.float32, jnp.bfloat16
    rates_ref, col_ref = refs[:2]
    pieces, refs = refs[2 : 2 + count], refs[2 + count :]
    held, refs = (refs[:2], refs[2:]) if more else (None, refs)
    outs, rows_ref = refs[:-1], refs[-1]
    width = col_ref.shape[1] - PAD
    n_rows = rows_ref.shape[0]

    turned, filled = [], 0
    for piece in pieces:
        rows_ref[filled : filled + piece.shape[0]] = piece[:, :width]
        filled += piece.shape[0]
        turned.append(piece[:, width:].astype(f32).T)
    turned = jnp.concatenate([value[:8] for value in turned], axis=1)
    row_sign = turned[0:1]
    row_norm = turned[1:2] + turned[2:3] + turned[3:4]

    scales = [rates_ref[band] * (-LOG2E / width) for band in range(rates_ref.shape[0])]
    step = min(256, col_ref.shape[0])
    for start in range(0, col_ref.shape[0], step):
        place = slice(start, start + step)
        col_z = col_ref[place, :width]
        tail = col_ref[place, width:].astype(f32)
        col_norm = tail[:, 1:2] + tail[:, 2:3] + tail[:, 3:4]
        cross = lax.dot_general(
            col_z, rows_ref[...], (((1,), (1,)), ((), ())), preferred_element_type=f32
        )
        dist = jnp.maximum(col_norm + row_norm - 2.0 * cross, 0.0)
        kernel = jnp.zeros((step, n_rows), f32)
        for band, scale in enumerate(scales):
            kernel += rates_ref[band] * jnp.exp2(scale * dist)
        kernel *= row_sign
        total = jnp.broadcast_to(jnp.sum(kernel, axis=1, keepdims=True), (step, PAD))
        other = jnp.dot(kernel.astype(bf16), rows_ref[...], preferred_element_type=f32)
        if more:
            total += held[0][place]
            other += held[1][place]
        if last:
            factor = (-32.0 / width) * tail[:, 0:1]
            wide = col_z.astype(f32)
            outs[0][place] = (factor * (total[:, :1] * wide - other)).astype(bf16)
        else:
            outs[0][place] = total
            outs[1][place] = other


def tiles(pieces, col, rates, held=(), last=False):
    f32, bf16 = jnp.float32, jnp.bfloat16
    n_cols, width = col.shape[0], col.shape[1] - PAD
    n_rows = sum(piece.shape[0] for piece in pieces)
    vmem = pl.BlockSpec(memory_space=pltpu.VMEM)
    if last:
        out_shape = jax.ShapeDtypeStruct((n_cols, width), bf16)
    else:
        out_shape = (
            jax.ShapeDtypeStruct((n_cols, PAD), f32),
            jax.ShapeDtypeStruct((n_cols, width), f32),
        )
    pairs = n_rows * n_cols
    return pl.pallas_call(
        functools.partial(tile_kernel, len(pieces), bool(held), last),
        out_shape=out_shape,
        in_specs=[pl.BlockSpec(memory_space=pltpu.SMEM)] + [vmem] * (1 + len(pieces) + len(held)),
        out_specs=vmem if last else (vmem, vmem),
        scratch_shapes=[pltpu.VMEM((n_rows, width), bf16)],
        compiler_params=pltpu.CompilerParams(vmem_limit_bytes=32 * 2**20),
        cost_estimate=pl.CostEstimate(
            flops=4 * pairs * width, bytes_accessed=4 * n_cols * width, transcendentals=5 * pairs
        ),
    )(rates, col, *pieces, *held)


def shards(features, w_proj, flags, rates):
    f32, bf16 = jnp.float32, jnp.bfloat16
    group = features.shape[0]
    width = w_proj.shape[1]
    n_row = lax.axis_size("row")
    n_col = lax.axis_size("col")
    half, quarter = group // 2, group // 4
    tpos = lax.axis_index("tensor")
    high, core = tpos // 2 == 1, tpos % 2 == 1

    def move(value, shift):
        return lax.ppermute(value, ZLINE, line_permutation(shift, n_row))

    def other_core(value):
        return move(value, lambda chip, core: (chip, 1 - core))

    away, kept = projection(jnp.reshape(tpos % 2, (1,)), features, w_proj)
    partial = (kept + other_core(away).astype(f32)).astype(bf16)
    far = move(partial, lambda chip, core: (chip + n_row, core))
    signs = (1 - 2 * flags).astype(f32).reshape(2, 2, quarter)
    s_half = pick(core, signs[:, 0], signs[:, 1]).reshape(half)
    block = whole_block(partial, far, jnp.broadcast_to(s_half[:, None], (half, PAD)))

    far_block = move(block, lambda chip, core: (chip + (n_row // 2) * (1 - 2 * core), core))
    pair = side_by_side(block, far_block, FLOPS)
    other_pair = other_core(pair)
    two_away = move(pair, lambda chip, core: (chip + 2 - 4 * core, core))
    next_own = move(pair, lambda chip, core: (chip + 1 - 2 * core, core))
    next_other = move(other_pair, lambda chip, core: (chip + 1 - 2 * core, core))
    own = pick(high, block[:quarter], block[quarter:])
    col = lax.all_to_all(
        jnp.broadcast_to(own[None], (n_col,) + own.shape), "col", 0, 0, tiled=True
    ).reshape(n_col * quarter, width + PAD)
    sums = tiles([pair, other_pair], col, rates)
    two_away = after(two_away, sums[0], 0)
    next_own = after(next_own, sums[0], 0)
    middle = [two_away, other_core(two_away), next_own, other_core(next_own)]
    sums = tiles(middle, col, rates, sums, False)
    next_other = after(next_other, middle[1], 0)
    part = tiles([next_other, other_core(next_other)], col, rates, sums, True)
    parts = lax.all_to_all(part.reshape(n_col, quarter, width), "col", 0, 0, tiled=True)
    grad = summed(parts)
    grad = lax.all_gather(grad, "tensor", axis=0, tiled=True)
    return result(grad, w_proj)


def solution(mesh):
    in_specs = (P(("row", "col"), "tensor"), P("tensor", None), P(("row", "col")), P())
    out_specs = P(("row", "col"), "tensor")
    return jax.shard_map(shards, mesh=mesh, in_specs=in_specs, out_specs=out_specs, check_vma=False)
```

```python
import functools
import math

import jax
import jax.numpy as jnp
from jax import lax
from jax.experimental import pallas as pl
from jax.experimental.pallas import tpu as pltpu
from jax.sharding import PartitionSpec as P

ZLINE = ("tensor", "row")
PAD = 128
LOG2E = math.log2(math.e)


def line_permutation(shift, n_row):
    length = 2 * n_row
    pairs = []
    for chip in range(length):
        for core in range(2):
            chip2, core2 = shift(chip, core)
            chip2 %= length
            source = ((chip // n_row) * 2 + core) * n_row + chip % n_row
            target = ((chip2 // n_row) * 2 + core2) * n_row + chip2 % n_row
            pairs.append((source, target))
    return pairs


def pick(second, low, high):
    return jnp.where(second, high, low)

CHUNKS = 4


def projection_kernel(core_ref, features_ref, w_ref, away_ref, kept_ref, rows, weights, total, sem):
    copies = []
    depth = rows.shape[1] // CHUNKS
    for index in range(CHUNKS):
        place = pl.ds(index * depth, depth)
        copies.append(
            (
                pltpu.make_async_copy(features_ref.at[:, place], rows.at[:, place], sem.at[0, index]),
                pltpu.make_async_copy(w_ref.at[place], weights.at[place], sem.at[1, index]),
            )
        )
        for copy in copies[-1]:
            copy.start()
    value = None
    for index in range(CHUNKS):
        place = slice(index * depth, (index + 1) * depth)
        for copy in copies[index]:
            copy.wait()
        term = jnp.dot(rows[:, place], weights[place], preferred_element_type=jnp.float32)
        value = term if value is None else value + term
    total[...] = value
    quarter = kept_ref.shape[0] // 2
    core = core_ref[0]
    for index in range(2):
        place = slice(index * quarter, (index + 1) * quarter)
        start = pl.multiple_of((2 * index + 1 - core) * quarter, quarter)
        away_ref[place] = total[pl.ds(start, quarter)].astype(away_ref.dtype)
        start = pl.multiple_of((2 * index + core) * quarter, quarter)
        kept_ref[place] = total[pl.ds(start, quarter)]


def projection(core, features, w_proj):
    rows, width = features.shape[0], w_proj.shape[1]
    vmem, anywhere = pl.BlockSpec(memory_space=pltpu.VMEM), pl.BlockSpec(memory_space=pl.ANY)
    return pl.pallas_call(
        projection_kernel,
        out_shape=(
            jax.ShapeDtypeStruct((rows // 2, width), jnp.bfloat16),
            jax.ShapeDtypeStruct((rows // 2, width), jnp.float32),
        ),
        in_specs=[pl.BlockSpec(memory_space=pltpu.SMEM), anywhere, anywhere],
        out_specs=(vmem, vmem),
        scratch_shapes=[
            pltpu.VMEM(features.shape, features.dtype),
            pltpu.VMEM(w_proj.shape, w_proj.dtype),
            pltpu.VMEM((rows, width), jnp.float32),
            pltpu.SemaphoreType.DMA((2, CHUNKS)),
        ],
        compiler_params=pltpu.CompilerParams(vmem_limit_bytes=60 * 2**20),
        cost_estimate=pl.CostEstimate(
            flops=2 * rows * width * w_proj.shape[0],
            bytes_accessed=2 * w_proj.shape[0] * width,
            transcendentals=0,
        ),
    )(core, features, w_proj)


def pair_kernel(gathered_ref, pair_ref):
    f32, bf16 = jnp.float32, jnp.bfloat16
    half = pair_ref.shape[0] // 2
    width = pair_ref.shape[1] - PAD
    for index in range(2):
        near = slice(index * half, (index + 1) * half)
        far = slice((index + 2) * half, (index + 3) * half)
        rows = gathered_ref[near, :width].astype(f32) + gathered_ref[far, :width].astype(f32)
        rows = rows.astype(bf16)
        pair_ref[near, :width] = rows
        norm = jnp.sum(jnp.square(rows.astype(f32)), axis=1, keepdims=True)
        first = norm.astype(bf16).astype(f32)
        second = (norm - first).astype(bf16).astype(f32)
        third = norm - first - second
        lane = lax.broadcasted_iota(jnp.int32, (half, PAD), 1)
        tail = jnp.where(lane == 1, first, jnp.where(lane == 2, second, third))
        sign = gathered_ref[near, width:].astype(f32)
        pair_ref[near, width:] = jnp.where(lane == 0, sign, tail).astype(bf16)


def whole_pair(gathered):
    vmem = pl.BlockSpec(memory_space=pltpu.VMEM)
    rows, columns = gathered.shape
    return pl.pallas_call(
        pair_kernel,
        out_shape=jax.ShapeDtypeStruct((rows // 2, columns), gathered.dtype),
        in_specs=[vmem],
        out_specs=vmem,
        compiler_params=pltpu.CompilerParams(vmem_limit_bytes=16 * 2**20),
        cost_estimate=pl.CostEstimate(
            flops=4 * rows * columns, bytes_accessed=3 * rows * columns, transcendentals=0
        ),
    )(gathered)


def result_kernel(grad_ref, w_ref, out_ref):
    out_ref[...] = lax.dot_general(
        grad_ref[...], w_ref[...], (((1,), (1,)), ((), ())), preferred_element_type=jnp.float32
    ).astype(out_ref.dtype)


def result(grad, w_proj):
    vmem = pl.BlockSpec(memory_space=pltpu.VMEM)
    rows, depth = grad.shape[0], w_proj.shape[0]
    return pl.pallas_call(
        result_kernel,
        out_shape=jax.ShapeDtypeStruct((rows, depth), grad.dtype),
        in_specs=[vmem] * 2,
        out_specs=vmem,
        compiler_params=pltpu.CompilerParams(vmem_limit_bytes=16 * 2**20),
        cost_estimate=pl.CostEstimate(
            flops=2 * rows * w_proj.size, bytes_accessed=2 * w_proj.size, transcendentals=0
        ),
    )(grad, w_proj)


def sum_kernel(parts_ref, out_ref):
    total = parts_ref[0].astype(jnp.float32)
    for index in range(1, parts_ref.shape[0]):
        total += parts_ref[index].astype(jnp.float32)
    out_ref[...] = total.astype(out_ref.dtype)


def summed(parts):
    vmem = pl.BlockSpec(memory_space=pltpu.VMEM)
    return pl.pallas_call(
        sum_kernel,
        out_shape=jax.ShapeDtypeStruct(parts.shape[1:], parts.dtype),
        in_specs=[vmem],
        out_specs=vmem,
        compiler_params=pltpu.CompilerParams(vmem_limit_bytes=16 * 2**20),
        cost_estimate=pl.CostEstimate(
            flops=parts.size, bytes_accessed=2 * parts.size, transcendentals=0
        ),
    )(parts)


def after_kernel(value_ref, first_ref, same_ref):
    pass


def after(value, first, flops):
    anywhere = pl.BlockSpec(memory_space=pl.ANY)
    return pl.pallas_call(
        after_kernel,
        out_shape=jax.ShapeDtypeStruct(value.shape, value.dtype),
        in_specs=[anywhere, anywhere],
        out_specs=anywhere,
        input_output_aliases={0: 0},
        compiler_params=pltpu.CompilerParams(vmem_limit_bytes=16 * 2**20),
        cost_estimate=pl.CostEstimate(flops=flops, bytes_accessed=0, transcendentals=0),
    )(value, first)


def tile_kernel(count, more, last, *refs):
    f32, bf16 = jnp.float32, jnp.bfloat16
    rates_ref, col_ref = refs[:2]
    pieces, refs = refs[2 : 2 + count], refs[2 + count :]
    held, refs = (refs[:2], refs[2:]) if more else (None, refs)
    outs, rows_ref = refs[:-1], refs[-1]
    width = col_ref.shape[1] - PAD
    n_rows = rows_ref.shape[0]

    turned, filled = [], 0
    for piece in pieces:
        rows_ref[filled : filled + piece.shape[0]] = piece[:, :width]
        filled += piece.shape[0]
        turned.append(piece[:, width:].astype(f32).T)
    turned = jnp.concatenate([value[:8] for value in turned], axis=1)
    row_sign = turned[0:1]
    row_norm = turned[1:2] + turned[2:3] + turned[3:4]

    scales = [rates_ref[band] * (-LOG2E / width) for band in range(rates_ref.shape[0])]
    step = min(256, col_ref.shape[0])
    for start in range(0, col_ref.shape[0], step):
        place = slice(start, start + step)
        col_z = col_ref[place, :width]
        tail = col_ref[place, width:].astype(f32)
        col_norm = tail[:, 1:2] + tail[:, 2:3] + tail[:, 3:4]
        cross = lax.dot_general(
            col_z, rows_ref[...], (((1,), (1,)), ((), ())), preferred_element_type=f32
        )
        dist = jnp.maximum(col_norm + row_norm - 2.0 * cross, 0.0)
        kernel = jnp.zeros((step, n_rows), f32)
        for band, scale in enumerate(scales):
            kernel += rates_ref[band] * jnp.exp2(scale * dist)
        kernel *= row_sign
        total = jnp.broadcast_to(jnp.sum(kernel, axis=1, keepdims=True), (step, PAD))
        other = jnp.dot(kernel.astype(bf16), rows_ref[...], preferred_element_type=f32)
        if more:
            total += held[0][place]
            other += held[1][place]
        if last:
            factor = (-32.0 / width) * tail[:, 0:1]
            wide = col_z.astype(f32)
            outs[0][place] = (factor * (total[:, :1] * wide - other)).astype(bf16)
        else:
            outs[0][place] = total
            outs[1][place] = other


def tiles(pieces, col, rates, held=(), last=False):
    f32, bf16 = jnp.float32, jnp.bfloat16
    n_cols, width = col.shape[0], col.shape[1] - PAD
    n_rows = sum(piece.shape[0] for piece in pieces)
    vmem = pl.BlockSpec(memory_space=pltpu.VMEM)
    if last:
        out_shape = jax.ShapeDtypeStruct((n_cols, width), bf16)
    else:
        out_shape = (
            jax.ShapeDtypeStruct((n_cols, PAD), f32),
            jax.ShapeDtypeStruct((n_cols, width), f32),
        )
    pairs = n_rows * n_cols
    return pl.pallas_call(
        functools.partial(tile_kernel, len(pieces), bool(held), last),
        out_shape=out_shape,
        in_specs=[pl.BlockSpec(memory_space=pltpu.SMEM)] + [vmem] * (1 + len(pieces) + len(held)),
        out_specs=vmem if last else (vmem, vmem),
        scratch_shapes=[pltpu.VMEM((n_rows, width), bf16)],
        compiler_params=pltpu.CompilerParams(vmem_limit_bytes=32 * 2**20),
        cost_estimate=pl.CostEstimate(
            flops=4 * pairs * width, bytes_accessed=4 * n_cols * width, transcendentals=5 * pairs
        ),
    )(rates, col, *pieces, *held)


def shards(features, w_proj, flags, rates):
    f32, bf16 = jnp.float32, jnp.bfloat16
    group = features.shape[0]
    width = w_proj.shape[1]
    n_row = lax.axis_size("row")
    n_col = lax.axis_size("col")
    half, quarter = group // 2, group // 4
    tpos = lax.axis_index("tensor")
    high, core = tpos // 2 == 1, tpos % 2 == 1

    def move(value, shift):
        return lax.ppermute(value, ZLINE, line_permutation(shift, n_row))

    def other_core(value):
        return move(value, lambda chip, core: (chip, 1 - core))

    away, kept = projection(jnp.reshape(tpos % 2, (1,)), features, w_proj)
    partial = (kept + other_core(away).astype(f32)).astype(bf16)
    signs = (1 - 2 * flags).astype(bf16).reshape(2, 2, quarter)
    s_half = pick(core, signs[:, 0], signs[:, 1]).reshape(half)
    signed = jnp.concatenate([partial, jnp.broadcast_to(s_half[:, None], (half, PAD))], axis=1)

    step = n_row // 2
    meeting = [
        [((chip // n_row) * 2 + side) * n_row + chip % n_row for chip in range(first, 2 * n_row, step)]
        for first in range(step)
        for side in range(2)
    ]
    gathered = lax.all_gather(signed, ZLINE, axis=0, tiled=True, axis_index_groups=meeting)
    pair = whole_pair(gathered)
    other_pair = other_core(pair)
    two_away = move(pair, lambda chip, core: (chip + 2 - 4 * core, core))
    next_own = move(pair, lambda chip, core: (chip + 1 - 2 * core, core))
    next_other = move(other_pair, lambda chip, core: (chip + 1 - 2 * core, core))
    place = jnp.where(lax.axis_index("row") < step, 0, half) + jnp.where(high, quarter, 0)
    own = lax.dynamic_slice_in_dim(pair, place, quarter, 0)
    col = lax.all_to_all(
        jnp.broadcast_to(own[None], (n_col,) + own.shape), "col", 0, 0, tiled=True
    ).reshape(n_col * quarter, width + PAD)
    sums = tiles([pair, other_pair], col, rates)
    two_away = after(two_away, sums[0], 0)
    next_own = after(next_own, sums[0], 0)
    middle = [two_away, other_core(two_away), next_own, other_core(next_own)]
    sums = tiles(middle, col, rates, sums, False)
    next_other = after(next_other, middle[1], 0)
    part = tiles([next_other, other_core(next_other)], col, rates, sums, True)
    parts = lax.all_to_all(part.reshape(n_col, quarter, width), "col", 0, 0, tiled=True)
    grad = summed(parts)
    grad = lax.all_gather(grad, "tensor", axis=0, tiled=True)
    return result(grad, w_proj)


def solution(mesh):
    in_specs = (P(("row", "col"), "tensor"), P("tensor", None), P(("row", "col")), P())
    out_specs = P(("row", "col"), "tensor")
    return jax.shard_map(shards, mesh=mesh, in_specs=in_specs, out_specs=out_specs, check_vma=False)
```

```python
import functools
import math

import jax
import jax.numpy as jnp
from jax import lax
from jax.experimental import pallas as pl
from jax.experimental.pallas import tpu as pltpu
from jax.sharding import PartitionSpec as P

ZLINE = ("tensor", "row")
PAD = 128
LOG2E = math.log2(math.e)
FLOPS = 4 * 10**10


def line_permutation(shift, n_row):
    length = 2 * n_row
    pairs = []
    for chip in range(length):
        for core in range(2):
            chip2, core2 = shift(chip, core)
            chip2 %= length
            source = ((chip // n_row) * 2 + core) * n_row + chip % n_row
            target = ((chip2 // n_row) * 2 + core2) * n_row + chip2 % n_row
            pairs.append((source, target))
    return pairs


def pick(second, low, high):
    return jnp.where(second, high, low)

CHUNKS = 4


def projection_kernel(core_ref, features_ref, w_ref, away_ref, kept_ref, rows, weights, total, sem):
    copies = []
    depth = rows.shape[1] // CHUNKS
    for index in range(CHUNKS):
        place = pl.ds(index * depth, depth)
        copies.append(
            (
                pltpu.make_async_copy(features_ref.at[:, place], rows.at[:, place], sem.at[0, index]),
                pltpu.make_async_copy(w_ref.at[place], weights.at[place], sem.at[1, index]),
            )
        )
        for copy in copies[-1]:
            copy.start()
    value = None
    for index in range(CHUNKS):
        place = slice(index * depth, (index + 1) * depth)
        for copy in copies[index]:
            copy.wait()
        term = jnp.dot(rows[:, place], weights[place], preferred_element_type=jnp.float32)
        value = term if value is None else value + term
    total[...] = value
    quarter = kept_ref.shape[0] // 2
    core = core_ref[0]
    for index in range(2):
        place = slice(index * quarter, (index + 1) * quarter)
        start = pl.multiple_of((2 * index + 1 - core) * quarter, quarter)
        away_ref[place] = total[pl.ds(start, quarter)].astype(away_ref.dtype)
        start = pl.multiple_of((2 * index + core) * quarter, quarter)
        kept_ref[place] = total[pl.ds(start, quarter)]


def projection(core, features, w_proj):
    rows, width = features.shape[0], w_proj.shape[1]
    vmem, anywhere = pl.BlockSpec(memory_space=pltpu.VMEM), pl.BlockSpec(memory_space=pl.ANY)
    return pl.pallas_call(
        projection_kernel,
        out_shape=(
            jax.ShapeDtypeStruct((rows // 2, width), jnp.bfloat16),
            jax.ShapeDtypeStruct((rows // 2, width), jnp.float32),
        ),
        in_specs=[pl.BlockSpec(memory_space=pltpu.SMEM), anywhere, anywhere],
        out_specs=(vmem, vmem),
        scratch_shapes=[
            pltpu.VMEM(features.shape, features.dtype),
            pltpu.VMEM(w_proj.shape, w_proj.dtype),
            pltpu.VMEM((rows, width), jnp.float32),
            pltpu.SemaphoreType.DMA((2, CHUNKS)),
        ],
        compiler_params=pltpu.CompilerParams(vmem_limit_bytes=60 * 2**20),
        cost_estimate=pl.CostEstimate(
            flops=2 * rows * width * w_proj.shape[0],
            bytes_accessed=2 * w_proj.shape[0] * width,
            transcendentals=0,
        ),
    )(core, features, w_proj)


def block_kernel(both_ref, signs_ref, block_ref):
    f32, bf16 = jnp.float32, jnp.bfloat16
    half, width = both_ref.shape[0] // 2, both_ref.shape[1]
    rows = (both_ref[:half].astype(f32) + both_ref[half:].astype(f32)).astype(bf16)
    block_ref[:, :width] = rows
    norm = jnp.sum(jnp.square(rows.astype(f32)), axis=1, keepdims=True)
    first = norm.astype(bf16).astype(f32)
    second = (norm - first).astype(bf16).astype(f32)
    third = norm - first - second
    lane = lax.broadcasted_iota(jnp.int32, (half, PAD), 1)
    tail = jnp.where(lane == 1, first, jnp.where(lane == 2, second, third))
    block_ref[:, width:] = jnp.where(lane == 0, signs_ref[...], tail).astype(bf16)


def whole_block(both, signs):
    vmem = pl.BlockSpec(memory_space=pltpu.VMEM)
    half, width = both.shape[0] // 2, both.shape[1]
    return pl.pallas_call(
        block_kernel,
        out_shape=jax.ShapeDtypeStruct((half, width + PAD), both.dtype),
        in_specs=[vmem] * 2,
        out_specs=vmem,
        compiler_params=pltpu.CompilerParams(vmem_limit_bytes=16 * 2**20),
        cost_estimate=pl.CostEstimate(
            flops=4 * half * width, bytes_accessed=6 * half * width, transcendentals=0
        ),
    )(both, signs)


def result_kernel(grad_ref, w_ref, out_ref):
    out_ref[...] = lax.dot_general(
        grad_ref[...], w_ref[...], (((1,), (1,)), ((), ())), preferred_element_type=jnp.float32
    ).astype(out_ref.dtype)


def result(grad, w_proj):
    vmem = pl.BlockSpec(memory_space=pltpu.VMEM)
    rows, depth = grad.shape[0], w_proj.shape[0]
    return pl.pallas_call(
        result_kernel,
        out_shape=jax.ShapeDtypeStruct((rows, depth), grad.dtype),
        in_specs=[vmem] * 2,
        out_specs=vmem,
        compiler_params=pltpu.CompilerParams(vmem_limit_bytes=16 * 2**20),
        cost_estimate=pl.CostEstimate(
            flops=2 * rows * w_proj.size, bytes_accessed=2 * w_proj.size, transcendentals=0
        ),
    )(grad, w_proj)


def sum_kernel(parts_ref, out_ref):
    total = parts_ref[0].astype(jnp.float32)
    for index in range(1, parts_ref.shape[0]):
        total += parts_ref[index].astype(jnp.float32)
    out_ref[...] = total.astype(out_ref.dtype)


def summed(parts):
    vmem = pl.BlockSpec(memory_space=pltpu.VMEM)
    return pl.pallas_call(
        sum_kernel,
        out_shape=jax.ShapeDtypeStruct(parts.shape[1:], parts.dtype),
        in_specs=[vmem],
        out_specs=vmem,
        compiler_params=pltpu.CompilerParams(vmem_limit_bytes=16 * 2**20),
        cost_estimate=pl.CostEstimate(
            flops=parts.size, bytes_accessed=2 * parts.size, transcendentals=0
        ),
    )(parts)


def pair_kernel(first_ref, second_ref, out_ref):
    half = first_ref.shape[0]
    out_ref[:half] = first_ref[...]
    out_ref[half:] = second_ref[...]


def side_by_side(first, second, flops):
    vmem = pl.BlockSpec(memory_space=pltpu.VMEM)
    return pl.pallas_call(
        pair_kernel,
        out_shape=jax.ShapeDtypeStruct((2 * first.shape[0], first.shape[1]), first.dtype),
        in_specs=[vmem, vmem],
        out_specs=vmem,
        compiler_params=pltpu.CompilerParams(vmem_limit_bytes=16 * 2**20),
        cost_estimate=pl.CostEstimate(flops=flops, bytes_accessed=0, transcendentals=0),
    )(first, second)


def after_kernel(value_ref, first_ref, same_ref):
    pass


def after(value, first, flops):
    anywhere = pl.BlockSpec(memory_space=pl.ANY)
    return pl.pallas_call(
        after_kernel,
        out_shape=jax.ShapeDtypeStruct(value.shape, value.dtype),
        in_specs=[anywhere, anywhere],
        out_specs=anywhere,
        input_output_aliases={0: 0},
        compiler_params=pltpu.CompilerParams(vmem_limit_bytes=16 * 2**20),
        cost_estimate=pl.CostEstimate(flops=flops, bytes_accessed=0, transcendentals=0),
    )(value, first)


def tile_kernel(count, more, last, *refs):
    f32, bf16 = jnp.float32, jnp.bfloat16
    rates_ref, col_ref = refs[:2]
    pieces, refs = refs[2 : 2 + count], refs[2 + count :]
    held, refs = (refs[:2], refs[2:]) if more else (None, refs)
    outs, rows_ref = refs[:-1], refs[-1]
    width = col_ref.shape[1] - PAD
    n_rows = rows_ref.shape[0]

    turned, filled = [], 0
    for piece in pieces:
        rows_ref[filled : filled + piece.shape[0]] = piece[:, :width]
        filled += piece.shape[0]
        turned.append(piece[:, width:].astype(f32).T)
    turned = jnp.concatenate([value[:8] for value in turned], axis=1)
    row_sign = turned[0:1]
    row_norm = turned[1:2] + turned[2:3] + turned[3:4]

    scales = [rates_ref[band] * (-LOG2E / width) for band in range(rates_ref.shape[0])]
    step = min(256, col_ref.shape[0])
    for start in range(0, col_ref.shape[0], step):
        place = slice(start, start + step)
        col_z = col_ref[place, :width]
        tail = col_ref[place, width:].astype(f32)
        col_norm = tail[:, 1:2] + tail[:, 2:3] + tail[:, 3:4]
        cross = lax.dot_general(
            col_z, rows_ref[...], (((1,), (1,)), ((), ())), preferred_element_type=f32
        )
        dist = jnp.maximum(col_norm + row_norm - 2.0 * cross, 0.0)
        kernel = jnp.zeros((step, n_rows), f32)
        for band, scale in enumerate(scales):
            kernel += rates_ref[band] * jnp.exp2(scale * dist)
        kernel *= row_sign
        total = jnp.broadcast_to(jnp.sum(kernel, axis=1, keepdims=True), (step, PAD))
        other = jnp.dot(kernel.astype(bf16), rows_ref[...], preferred_element_type=f32)
        if more:
            total += held[0][place]
            other += held[1][place]
        if last:
            factor = (-32.0 / width) * tail[:, 0:1]
            wide = col_z.astype(f32)
            outs[0][place] = (factor * (total[:, :1] * wide - other)).astype(bf16)
        else:
            outs[0][place] = total
            outs[1][place] = other


def tiles(pieces, col, rates, held=(), last=False):
    f32, bf16 = jnp.float32, jnp.bfloat16
    n_cols, width = col.shape[0], col.shape[1] - PAD
    n_rows = sum(piece.shape[0] for piece in pieces)
    vmem = pl.BlockSpec(memory_space=pltpu.VMEM)
    if last:
        out_shape = jax.ShapeDtypeStruct((n_cols, width), bf16)
    else:
        out_shape = (
            jax.ShapeDtypeStruct((n_cols, PAD), f32),
            jax.ShapeDtypeStruct((n_cols, width), f32),
        )
    pairs = n_rows * n_cols
    return pl.pallas_call(
        functools.partial(tile_kernel, len(pieces), bool(held), last),
        out_shape=out_shape,
        in_specs=[pl.BlockSpec(memory_space=pltpu.SMEM)] + [vmem] * (1 + len(pieces) + len(held)),
        out_specs=vmem if last else (vmem, vmem),
        scratch_shapes=[pltpu.VMEM((n_rows, width), bf16)],
        compiler_params=pltpu.CompilerParams(vmem_limit_bytes=32 * 2**20),
        cost_estimate=pl.CostEstimate(
            flops=4 * pairs * width, bytes_accessed=4 * n_cols * width, transcendentals=5 * pairs
        ),
    )(rates, col, *pieces, *held)


def shards(features, w_proj, flags, rates):
    f32, bf16 = jnp.float32, jnp.bfloat16
    group = features.shape[0]
    width = w_proj.shape[1]
    n_row = lax.axis_size("row")
    n_col = lax.axis_size("col")
    half, quarter = group // 2, group // 4
    tpos = lax.axis_index("tensor")
    high, core = tpos // 2 == 1, tpos % 2 == 1

    def move(value, shift):
        return lax.ppermute(value, ZLINE, line_permutation(shift, n_row))

    def other_core(value):
        return move(value, lambda chip, core: (chip, 1 - core))

    away, kept = projection(jnp.reshape(tpos % 2, (1,)), features, w_proj)
    partial = (kept + other_core(away).astype(f32)).astype(bf16)
    holders = [
        [(side + 2 * end) * n_row + row for end in range(2)] for row in range(n_row) for side in range(2)
    ]
    both = lax.all_gather(partial, ZLINE, axis=0, tiled=True, axis_index_groups=holders)
    signs = (1 - 2 * flags).astype(f32).reshape(2, 2, quarter)
    s_half = pick(core, signs[:, 0], signs[:, 1]).reshape(half)
    block = whole_block(both, jnp.broadcast_to(s_half[:, None], (half, PAD)))

    far_block = move(block, lambda chip, core: (chip + (n_row // 2) * (1 - 2 * core), core))
    pair = side_by_side(block, far_block, FLOPS)
    other_pair = other_core(pair)
    two_away = move(pair, lambda chip, core: (chip + 2 - 4 * core, core))
    next_own = move(pair, lambda chip, core: (chip + 1 - 2 * core, core))
    next_other = move(other_pair, lambda chip, core: (chip + 1 - 2 * core, core))
    own = pick(high, block[:quarter], block[quarter:])
    col = lax.all_to_all(
        jnp.broadcast_to(own[None], (n_col,) + own.shape), "col", 0, 0, tiled=True
    ).reshape(n_col * quarter, width + PAD)
    sums = tiles([pair, other_pair], col, rates)
    two_away = after(two_away, sums[0], 0)
    next_own = after(next_own, sums[0], 0)
    middle = [two_away, other_core(two_away), next_own, other_core(next_own)]
    sums = tiles(middle, col, rates, sums, False)
    next_other = after(next_other, middle[1], 0)
    part = tiles([next_other, other_core(next_other)], col, rates, sums, True)
    parts = lax.all_to_all(part.reshape(n_col, quarter, width), "col", 0, 0, tiled=True)
    grad = summed(parts)
    grad = lax.all_gather(grad, "tensor", axis=0, tiled=True)
    return result(grad, w_proj)


def solution(mesh):
    in_specs = (P(("row", "col"), "tensor"), P("tensor", None), P(("row", "col")), P())
    out_specs = P(("row", "col"), "tensor")
    return jax.shard_map(shards, mesh=mesh, in_specs=in_specs, out_specs=out_specs, check_vma=False)
```

```python
import functools
import math

import jax
import jax.numpy as jnp
from jax import lax
from jax.experimental import pallas as pl
from jax.experimental.pallas import tpu as pltpu
from jax.sharding import PartitionSpec as P

ZLINE = ("tensor", "row")
PAD = 128
LOG2E = math.log2(math.e)
FLOPS = 4 * 10**10


def line_permutation(shift, n_row):
    length = 2 * n_row
    pairs = []
    for chip in range(length):
        for core in range(2):
            chip2, core2 = shift(chip, core)
            chip2 %= length
            source = ((chip // n_row) * 2 + core) * n_row + chip % n_row
            target = ((chip2 // n_row) * 2 + core2) * n_row + chip2 % n_row
            pairs.append((source, target))
    return pairs


def pick(second, low, high):
    return jnp.where(second, high, low)

CHUNKS = 4


def projection_kernel(core_ref, features_ref, w_ref, away_ref, kept_ref, rows, weights, total, sem):
    copies = []
    depth = rows.shape[1] // CHUNKS
    for index in range(CHUNKS):
        place = pl.ds(index * depth, depth)
        copies.append(
            (
                pltpu.make_async_copy(features_ref.at[:, place], rows.at[:, place], sem.at[0, index]),
                pltpu.make_async_copy(w_ref.at[place], weights.at[place], sem.at[1, index]),
            )
        )
        for copy in copies[-1]:
            copy.start()
    value = None
    for index in range(CHUNKS):
        place = slice(index * depth, (index + 1) * depth)
        for copy in copies[index]:
            copy.wait()
        term = jnp.dot(rows[:, place], weights[place], preferred_element_type=jnp.float32)
        value = term if value is None else value + term
    total[...] = value
    quarter = kept_ref.shape[0] // 2
    core = core_ref[0]
    for index in range(2):
        place = slice(index * quarter, (index + 1) * quarter)
        start = pl.multiple_of((2 * index + 1 - core) * quarter, quarter)
        away_ref[place] = total[pl.ds(start, quarter)].astype(away_ref.dtype)
        start = pl.multiple_of((2 * index + core) * quarter, quarter)
        kept_ref[place] = total[pl.ds(start, quarter)]


def projection(core, features, w_proj):
    rows, width = features.shape[0], w_proj.shape[1]
    vmem, anywhere = pl.BlockSpec(memory_space=pltpu.VMEM), pl.BlockSpec(memory_space=pl.ANY)
    return pl.pallas_call(
        projection_kernel,
        out_shape=(
            jax.ShapeDtypeStruct((rows // 2, width), jnp.bfloat16),
            jax.ShapeDtypeStruct((rows // 2, width), jnp.float32),
        ),
        in_specs=[pl.BlockSpec(memory_space=pltpu.SMEM), anywhere, anywhere],
        out_specs=(vmem, vmem),
        scratch_shapes=[
            pltpu.VMEM(features.shape, features.dtype),
            pltpu.VMEM(w_proj.shape, w_proj.dtype),
            pltpu.VMEM((rows, width), jnp.float32),
            pltpu.SemaphoreType.DMA((2, CHUNKS)),
        ],
        compiler_params=pltpu.CompilerParams(vmem_limit_bytes=60 * 2**20),
        cost_estimate=pl.CostEstimate(
            flops=2 * rows * width * w_proj.shape[0],
            bytes_accessed=2 * w_proj.shape[0] * width,
            transcendentals=0,
        ),
    )(core, features, w_proj)


def block_kernel(both_ref, signs_ref, block_ref):
    f32, bf16 = jnp.float32, jnp.bfloat16
    half, width = both_ref.shape[0] // 2, both_ref.shape[1]
    rows = (both_ref[:half].astype(f32) + both_ref[half:].astype(f32)).astype(bf16)
    block_ref[:, :width] = rows
    norm = jnp.sum(jnp.square(rows.astype(f32)), axis=1, keepdims=True)
    first = norm.astype(bf16).astype(f32)
    second = (norm - first).astype(bf16).astype(f32)
    third = norm - first - second
    lane = lax.broadcasted_iota(jnp.int32, (half, PAD), 1)
    tail = jnp.where(lane == 1, first, jnp.where(lane == 2, second, third))
    block_ref[:, width:] = jnp.where(lane == 0, signs_ref[...], tail).astype(bf16)


def whole_block(both, signs):
    vmem = pl.BlockSpec(memory_space=pltpu.VMEM)
    half, width = both.shape[0] // 2, both.shape[1]
    return pl.pallas_call(
        block_kernel,
        out_shape=jax.ShapeDtypeStruct((half, width + PAD), both.dtype),
        in_specs=[vmem] * 2,
        out_specs=vmem,
        compiler_params=pltpu.CompilerParams(vmem_limit_bytes=16 * 2**20),
        cost_estimate=pl.CostEstimate(
            flops=4 * half * width, bytes_accessed=6 * half * width, transcendentals=0
        ),
    )(both, signs)


def result_kernel(grad_ref, w_ref, out_ref):
    out_ref[...] = lax.dot_general(
        grad_ref[...], w_ref[...], (((1,), (1,)), ((), ())), preferred_element_type=jnp.float32
    ).astype(out_ref.dtype)


def result(grad, w_proj):
    vmem = pl.BlockSpec(memory_space=pltpu.VMEM)
    rows, depth = grad.shape[0], w_proj.shape[0]
    return pl.pallas_call(
        result_kernel,
        out_shape=jax.ShapeDtypeStruct((rows, depth), grad.dtype),
        in_specs=[vmem] * 2,
        out_specs=vmem,
        compiler_params=pltpu.CompilerParams(vmem_limit_bytes=16 * 2**20),
        cost_estimate=pl.CostEstimate(
            flops=2 * rows * w_proj.size, bytes_accessed=2 * w_proj.size, transcendentals=0
        ),
    )(grad, w_proj)


def sum_kernel(parts_ref, out_ref):
    total = parts_ref[0].astype(jnp.float32)
    for index in range(1, parts_ref.shape[0]):
        total += parts_ref[index].astype(jnp.float32)
    out_ref[...] = total.astype(out_ref.dtype)


def summed(parts):
    vmem = pl.BlockSpec(memory_space=pltpu.VMEM)
    return pl.pallas_call(
        sum_kernel,
        out_shape=jax.ShapeDtypeStruct(parts.shape[1:], parts.dtype),
        in_specs=[vmem],
        out_specs=vmem,
        compiler_params=pltpu.CompilerParams(vmem_limit_bytes=16 * 2**20),
        cost_estimate=pl.CostEstimate(
            flops=parts.size, bytes_accessed=2 * parts.size, transcendentals=0
        ),
    )(parts)


def pair_kernel(first_ref, second_ref, out_ref):
    half = first_ref.shape[0]
    out_ref[:half] = first_ref[...]
    out_ref[half:] = second_ref[...]


def side_by_side(first, second, flops):
    vmem = pl.BlockSpec(memory_space=pltpu.VMEM)
    return pl.pallas_call(
        pair_kernel,
        out_shape=jax.ShapeDtypeStruct((2 * first.shape[0], first.shape[1]), first.dtype),
        in_specs=[vmem, vmem],
        out_specs=vmem,
        compiler_params=pltpu.CompilerParams(vmem_limit_bytes=16 * 2**20),
        cost_estimate=pl.CostEstimate(flops=flops, bytes_accessed=0, transcendentals=0),
    )(first, second)


def after_kernel(value_ref, first_ref, same_ref):
    pass


def after(value, first, flops):
    anywhere = pl.BlockSpec(memory_space=pl.ANY)
    return pl.pallas_call(
        after_kernel,
        out_shape=jax.ShapeDtypeStruct(value.shape, value.dtype),
        in_specs=[anywhere, anywhere],
        out_specs=anywhere,
        input_output_aliases={0: 0},
        compiler_params=pltpu.CompilerParams(vmem_limit_bytes=16 * 2**20),
        cost_estimate=pl.CostEstimate(flops=flops, bytes_accessed=0, transcendentals=0),
    )(value, first)


def tile_kernel(count, more, last, *refs):
    f32, bf16 = jnp.float32, jnp.bfloat16
    rates_ref, col_ref = refs[:2]
    pieces, refs = refs[2 : 2 + count], refs[2 + count :]
    held, refs = (refs[:2], refs[2:]) if more else (None, refs)
    outs, rows_ref = refs[:-1], refs[-1]
    width = col_ref.shape[1] - PAD
    n_rows = rows_ref.shape[0]

    turned, filled = [], 0
    for piece in pieces:
        rows_ref[filled : filled + piece.shape[0]] = piece[:, :width]
        filled += piece.shape[0]
        turned.append(piece[:, width:].astype(f32).T)
    turned = jnp.concatenate([value[:8] for value in turned], axis=1)
    row_sign = turned[0:1]
    row_norm = turned[1:2] + turned[2:3] + turned[3:4]

    scales = [rates_ref[band] * (-LOG2E / width) for band in range(rates_ref.shape[0])]
    step = min(256, col_ref.shape[0])
    for start in range(0, col_ref.shape[0], step):
        place = slice(start, start + step)
        col_z = col_ref[place, :width]
        tail = col_ref[place, width:].astype(f32)
        col_norm = tail[:, 1:2] + tail[:, 2:3] + tail[:, 3:4]
        cross = lax.dot_general(
            col_z, rows_ref[...], (((1,), (1,)), ((), ())), preferred_element_type=f32
        )
        dist = jnp.maximum(col_norm + row_norm - 2.0 * cross, 0.0)
        kernel = jnp.zeros((step, n_rows), f32)
        for band, scale in enumerate(scales):
            kernel += rates_ref[band] * jnp.exp2(scale * dist)
        kernel *= row_sign
        total = jnp.broadcast_to(jnp.sum(kernel, axis=1, keepdims=True), (step, PAD))
        other = jnp.dot(kernel.astype(bf16), rows_ref[...], preferred_element_type=f32)
        if more:
            total += held[0][place]
            other += held[1][place]
        if last:
            factor = (-32.0 / width) * tail[:, 0:1]
            wide = col_z.astype(f32)
            outs[0][place] = (factor * (total[:, :1] * wide - other)).astype(bf16)
        else:
            outs[0][place] = total
            outs[1][place] = other


def tiles(pieces, col, rates, held=(), last=False):
    f32, bf16 = jnp.float32, jnp.bfloat16
    n_cols, width = col.shape[0], col.shape[1] - PAD
    n_rows = sum(piece.shape[0] for piece in pieces)
    vmem = pl.BlockSpec(memory_space=pltpu.VMEM)
    if last:
        out_shape = jax.ShapeDtypeStruct((n_cols, width), bf16)
    else:
        out_shape = (
            jax.ShapeDtypeStruct((n_cols, PAD), f32),
            jax.ShapeDtypeStruct((n_cols, width), f32),
        )
    pairs = n_rows * n_cols
    return pl.pallas_call(
        functools.partial(tile_kernel, len(pieces), bool(held), last),
        out_shape=out_shape,
        in_specs=[pl.BlockSpec(memory_space=pltpu.SMEM)] + [vmem] * (1 + len(pieces) + len(held)),
        out_specs=vmem if last else (vmem, vmem),
        scratch_shapes=[pltpu.VMEM((n_rows, width), bf16)],
        compiler_params=pltpu.CompilerParams(vmem_limit_bytes=32 * 2**20),
        cost_estimate=pl.CostEstimate(
            flops=4 * pairs * width, bytes_accessed=4 * n_cols * width, transcendentals=5 * pairs
        ),
    )(rates, col, *pieces, *held)


def shards(features, w_proj, flags, rates):
    f32, bf16 = jnp.float32, jnp.bfloat16
    group = features.shape[0]
    width = w_proj.shape[1]
    n_row = lax.axis_size("row")
    n_col = lax.axis_size("col")
    half, quarter = group // 2, group // 4
    tpos = lax.axis_index("tensor")
    high, core = tpos // 2 == 1, tpos % 2 == 1

    def move(value, shift):
        return lax.ppermute(value, ZLINE, line_permutation(shift, n_row))

    def other_core(value):
        return move(value, lambda chip, core: (chip, 1 - core))

    away, kept = projection(jnp.reshape(tpos % 2, (1,)), features, w_proj)
    partial = (kept + other_core(away).astype(f32)).astype(bf16)
    holders = [
        [(side + 2 * end) * n_row + row for end in range(2)] for row in range(n_row) for side in range(2)
    ]
    both = lax.all_gather(partial, ZLINE, axis=0, tiled=True, axis_index_groups=holders)
    signs = (1 - 2 * flags).astype(f32).reshape(2, 2, quarter)
    s_half = pick(core, signs[:, 0], signs[:, 1]).reshape(half)
    block = whole_block(both, jnp.broadcast_to(s_half[:, None], (half, PAD)))

    far_block = move(block, lambda chip, core: (chip + (n_row // 2) * (1 - 2 * core), core))
    pair = side_by_side(block, far_block, FLOPS)
    other_pair = other_core(pair)
    two_away = move(pair, lambda chip, core: (chip + 2 - 4 * core, core))
    next_own = move(pair, lambda chip, core: (chip + 1 - 2 * core, core))
    next_other = move(other_pair, lambda chip, core: (chip + 1 - 2 * core, core))
    own = pick(high, block[:quarter], block[quarter:])
    col = lax.all_to_all(
        jnp.broadcast_to(own[None], (n_col,) + own.shape), "col", 0, 0, tiled=True
    ).reshape(n_col * quarter, width + PAD)
    gate = after(other_pair, pair, FLOPS // 100)
    two_away = after(two_away, gate, 0)
    next_own = after(next_own, gate, 0)
    middle = [two_away, other_core(two_away), next_own, other_core(next_own)]
    sums = tiles([pair, gate] + middle, col, rates)
    next_other = after(next_other, middle[1], 0)
    part = tiles([next_other, other_core(next_other)], col, rates, sums, True)
    parts = lax.all_to_all(part.reshape(n_col, quarter, width), "col", 0, 0, tiled=True)
    grad = summed(parts)
    grad = lax.all_gather(grad, "tensor", axis=0, tiled=True)
    return result(grad, w_proj)


def solution(mesh):
    in_specs = (P(("row", "col"), "tensor"), P("tensor", None), P(("row", "col")), P())
    out_specs = P(("row", "col"), "tensor")
    return jax.shard_map(shards, mesh=mesh, in_specs=in_specs, out_specs=out_specs, check_vma=False)
```

```python
import functools
import math

import jax
import jax.numpy as jnp
from jax import lax
from jax.experimental import pallas as pl
from jax.experimental.pallas import tpu as pltpu
from jax.sharding import PartitionSpec as P

ZLINE = ("tensor", "row")
PAD = 128
LOG2E = math.log2(math.e)
FLOPS = 4 * 10**10


def line_permutation(shift, n_row):
    length = 2 * n_row
    pairs = []
    for chip in range(length):
        for core in range(2):
            chip2, core2 = shift(chip, core)
            chip2 %= length
            source = ((chip // n_row) * 2 + core) * n_row + chip % n_row
            target = ((chip2 // n_row) * 2 + core2) * n_row + chip2 % n_row
            pairs.append((source, target))
    return pairs


def pick(second, low, high):
    return jnp.where(second, high, low)

CHUNKS = 6


def projection_kernel(core_ref, features_ref, w_ref, away_ref, kept_ref, rows, weights, total, sem):
    copies = []
    depth = rows.shape[1] // CHUNKS
    for index in range(CHUNKS):
        place = pl.ds(index * depth, depth)
        copies.append(
            (
                pltpu.make_async_copy(features_ref.at[:, place], rows.at[:, place], sem.at[0, index]),
                pltpu.make_async_copy(w_ref.at[place], weights.at[place], sem.at[1, index]),
            )
        )
        for copy in copies[-1]:
            copy.start()
    value = None
    for index in range(CHUNKS):
        place = slice(index * depth, (index + 1) * depth)
        for copy in copies[index]:
            copy.wait()
        term = jnp.dot(rows[:, place], weights[place], preferred_element_type=jnp.float32)
        value = term if value is None else value + term
    total[...] = value
    quarter = kept_ref.shape[0] // 2
    core = core_ref[0]
    for index in range(2):
        place = slice(index * quarter, (index + 1) * quarter)
        start = pl.multiple_of((2 * index + 1 - core) * quarter, quarter)
        away_ref[place] = total[pl.ds(start, quarter)].astype(away_ref.dtype)
        start = pl.multiple_of((2 * index + core) * quarter, quarter)
        kept_ref[place] = total[pl.ds(start, quarter)]


def projection(core, features, w_proj):
    rows, width = features.shape[0], w_proj.shape[1]
    vmem, anywhere = pl.BlockSpec(memory_space=pltpu.VMEM), pl.BlockSpec(memory_space=pl.ANY)
    return pl.pallas_call(
        projection_kernel,
        out_shape=(
            jax.ShapeDtypeStruct((rows // 2, width), jnp.bfloat16),
            jax.ShapeDtypeStruct((rows // 2, width), jnp.float32),
        ),
        in_specs=[pl.BlockSpec(memory_space=pltpu.SMEM), anywhere, anywhere],
        out_specs=(vmem, vmem),
        scratch_shapes=[
            pltpu.VMEM(features.shape, features.dtype),
            pltpu.VMEM(w_proj.shape, w_proj.dtype),
            pltpu.VMEM((rows, width), jnp.float32),
            pltpu.SemaphoreType.DMA((2, CHUNKS)),
        ],
        compiler_params=pltpu.CompilerParams(vmem_limit_bytes=60 * 2**20),
        cost_estimate=pl.CostEstimate(
            flops=2 * rows * width * w_proj.shape[0],
            bytes_accessed=2 * w_proj.shape[0] * width,
            transcendentals=0,
        ),
    )(core, features, w_proj)


def block_kernel(both_ref, signs_ref, block_ref):
    f32, bf16 = jnp.float32, jnp.bfloat16
    half, width = both_ref.shape[0] // 2, both_ref.shape[1]
    rows = (both_ref[:half].astype(f32) + both_ref[half:].astype(f32)).astype(bf16)
    block_ref[:, :width] = rows
    norm = jnp.sum(jnp.square(rows.astype(f32)), axis=1, keepdims=True)
    first = norm.astype(bf16).astype(f32)
    second = (norm - first).astype(bf16).astype(f32)
    third = norm - first - second
    lane = lax.broadcasted_iota(jnp.int32, (half, PAD), 1)
    tail = jnp.where(lane == 1, first, jnp.where(lane == 2, second, third))
    block_ref[:, width:] = jnp.where(lane == 0, signs_ref[...], tail).astype(bf16)


def whole_block(both, signs):
    vmem = pl.BlockSpec(memory_space=pltpu.VMEM)
    half, width = both.shape[0] // 2, both.shape[1]
    return pl.pallas_call(
        block_kernel,
        out_shape=jax.ShapeDtypeStruct((half, width + PAD), both.dtype),
        in_specs=[vmem] * 2,
        out_specs=vmem,
        compiler_params=pltpu.CompilerParams(vmem_limit_bytes=16 * 2**20),
        cost_estimate=pl.CostEstimate(
            flops=4 * half * width, bytes_accessed=6 * half * width, transcendentals=0
        ),
    )(both, signs)


def result_kernel(grad_ref, w_ref, out_ref):
    out_ref[...] = lax.dot_general(
        grad_ref[...], w_ref[...], (((1,), (1,)), ((), ())), preferred_element_type=jnp.float32
    ).astype(out_ref.dtype)


def result(grad, w_proj):
    vmem = pl.BlockSpec(memory_space=pltpu.VMEM)
    rows, depth = grad.shape[0], w_proj.shape[0]
    return pl.pallas_call(
        result_kernel,
        out_shape=jax.ShapeDtypeStruct((rows, depth), grad.dtype),
        in_specs=[vmem] * 2,
        out_specs=vmem,
        compiler_params=pltpu.CompilerParams(vmem_limit_bytes=16 * 2**20),
        cost_estimate=pl.CostEstimate(
            flops=2 * rows * w_proj.size, bytes_accessed=2 * w_proj.size, transcendentals=0
        ),
    )(grad, w_proj)


def sum_kernel(parts_ref, out_ref):
    total = parts_ref[0].astype(jnp.float32)
    for index in range(1, parts_ref.shape[0]):
        total += parts_ref[index].astype(jnp.float32)
    out_ref[...] = total.astype(out_ref.dtype)


def summed(parts):
    vmem = pl.BlockSpec(memory_space=pltpu.VMEM)
    return pl.pallas_call(
        sum_kernel,
        out_shape=jax.ShapeDtypeStruct(parts.shape[1:], parts.dtype),
        in_specs=[vmem],
        out_specs=vmem,
        compiler_params=pltpu.CompilerParams(vmem_limit_bytes=16 * 2**20),
        cost_estimate=pl.CostEstimate(
            flops=parts.size, bytes_accessed=2 * parts.size, transcendentals=0
        ),
    )(parts)


def pair_kernel(first_ref, second_ref, out_ref):
    half = first_ref.shape[0]
    out_ref[:half] = first_ref[...]
    out_ref[half:] = second_ref[...]


def side_by_side(first, second, flops):
    vmem = pl.BlockSpec(memory_space=pltpu.VMEM)
    return pl.pallas_call(
        pair_kernel,
        out_shape=jax.ShapeDtypeStruct((2 * first.shape[0], first.shape[1]), first.dtype),
        in_specs=[vmem, vmem],
        out_specs=vmem,
        compiler_params=pltpu.CompilerParams(vmem_limit_bytes=16 * 2**20),
        cost_estimate=pl.CostEstimate(flops=flops, bytes_accessed=0, transcendentals=0),
    )(first, second)


def after_kernel(value_ref, first_ref, same_ref):
    pass


def after(value, first, flops):
    anywhere = pl.BlockSpec(memory_space=pl.ANY)
    return pl.pallas_call(
        after_kernel,
        out_shape=jax.ShapeDtypeStruct(value.shape, value.dtype),
        in_specs=[anywhere, anywhere],
        out_specs=anywhere,
        input_output_aliases={0: 0},
        compiler_params=pltpu.CompilerParams(vmem_limit_bytes=16 * 2**20),
        cost_estimate=pl.CostEstimate(flops=flops, bytes_accessed=0, transcendentals=0),
    )(value, first)


def tile_kernel(count, more, last, *refs):
    f32, bf16 = jnp.float32, jnp.bfloat16
    rates_ref, col_ref = refs[:2]
    pieces, refs = refs[2 : 2 + count], refs[2 + count :]
    held, refs = (refs[:2], refs[2:]) if more else (None, refs)
    outs, rows_ref = refs[:-1], refs[-1]
    width = col_ref.shape[1] - PAD
    n_rows = rows_ref.shape[0]

    turned, filled = [], 0
    for piece in pieces:
        rows_ref[filled : filled + piece.shape[0]] = piece[:, :width]
        filled += piece.shape[0]
        turned.append(piece[:, width:].astype(f32).T)
    turned = jnp.concatenate([value[:8] for value in turned], axis=1)
    row_sign = turned[0:1]
    row_norm = turned[1:2] + turned[2:3] + turned[3:4]

    scales = [rates_ref[band] * (-LOG2E / width) for band in range(rates_ref.shape[0])]
    step = min(256, col_ref.shape[0])
    for start in range(0, col_ref.shape[0], step):
        place = slice(start, start + step)
        col_z = col_ref[place, :width]
        tail = col_ref[place, width:].astype(f32)
        col_norm = tail[:, 1:2] + tail[:, 2:3] + tail[:, 3:4]
        cross = lax.dot_general(
            col_z, rows_ref[...], (((1,), (1,)), ((), ())), preferred_element_type=f32
        )
        dist = jnp.maximum(col_norm + row_norm - 2.0 * cross, 0.0)
        kernel = jnp.zeros((step, n_rows), f32)
        for band, scale in enumerate(scales):
            kernel += rates_ref[band] * jnp.exp2(scale * dist)
        kernel *= row_sign
        total = jnp.broadcast_to(jnp.sum(kernel, axis=1, keepdims=True), (step, PAD))
        other = jnp.dot(kernel.astype(bf16), rows_ref[...], preferred_element_type=f32)
        if more:
            total += held[0][place]
            other += held[1][place]
        if last:
            factor = (-32.0 / width) * tail[:, 0:1]
            wide = col_z.astype(f32)
            outs[0][place] = (factor * (total[:, :1] * wide - other)).astype(bf16)
        else:
            outs[0][place] = total
            outs[1][place] = other


def tiles(pieces, col, rates, held=(), last=False):
    f32, bf16 = jnp.float32, jnp.bfloat16
    n_cols, width = col.shape[0], col.shape[1] - PAD
    n_rows = sum(piece.shape[0] for piece in pieces)
    vmem = pl.BlockSpec(memory_space=pltpu.VMEM)
    if last:
        out_shape = jax.ShapeDtypeStruct((n_cols, width), bf16)
    else:
        out_shape = (
            jax.ShapeDtypeStruct((n_cols, PAD), f32),
            jax.ShapeDtypeStruct((n_cols, width), f32),
        )
    pairs = n_rows * n_cols
    return pl.pallas_call(
        functools.partial(tile_kernel, len(pieces), bool(held), last),
        out_shape=out_shape,
        in_specs=[pl.BlockSpec(memory_space=pltpu.SMEM)] + [vmem] * (1 + len(pieces) + len(held)),
        out_specs=vmem if last else (vmem, vmem),
        scratch_shapes=[pltpu.VMEM((n_rows, width), bf16)],
        compiler_params=pltpu.CompilerParams(vmem_limit_bytes=32 * 2**20),
        cost_estimate=pl.CostEstimate(
            flops=4 * pairs * width, bytes_accessed=4 * n_cols * width, transcendentals=5 * pairs
        ),
    )(rates, col, *pieces, *held)


def shards(features, w_proj, flags, rates):
    f32, bf16 = jnp.float32, jnp.bfloat16
    group = features.shape[0]
    width = w_proj.shape[1]
    n_row = lax.axis_size("row")
    n_col = lax.axis_size("col")
    half, quarter = group // 2, group // 4
    tpos = lax.axis_index("tensor")
    high, core = tpos // 2 == 1, tpos % 2 == 1

    def move(value, shift):
        return lax.ppermute(value, ZLINE, line_permutation(shift, n_row))

    def other_core(value):
        return move(value, lambda chip, core: (chip, 1 - core))

    away, kept = projection(jnp.reshape(tpos % 2, (1,)), features, w_proj)
    partial = (kept + other_core(away).astype(f32)).astype(bf16)
    holders = [
        [(side + 2 * end) * n_row + row for end in range(2)] for row in range(n_row) for side in range(2)
    ]
    both = lax.all_gather(partial, ZLINE, axis=0, tiled=True, axis_index_groups=holders)
    signs = (1 - 2 * flags).astype(f32).reshape(2, 2, quarter)
    s_half = pick(core, signs[:, 0], signs[:, 1]).reshape(half)
    block = whole_block(both, jnp.broadcast_to(s_half[:, None], (half, PAD)))

    far_block = move(block, lambda chip, core: (chip + (n_row // 2) * (1 - 2 * core), core))
    pair = side_by_side(block, far_block, FLOPS)
    other_pair = other_core(pair)
    two_away = move(pair, lambda chip, core: (chip + 2 - 4 * core, core))
    next_own = move(pair, lambda chip, core: (chip + 1 - 2 * core, core))
    next_other = move(other_pair, lambda chip, core: (chip + 1 - 2 * core, core))
    own = pick(high, block[:quarter], block[quarter:])
    col = lax.all_to_all(
        jnp.broadcast_to(own[None], (n_col,) + own.shape), "col", 0, 0, tiled=True
    ).reshape(n_col * quarter, width + PAD)
    sums = tiles([pair, other_pair], col, rates)
    two_away = after(two_away, sums[0], 0)
    next_own = after(next_own, sums[0], 0)
    middle = [two_away, other_core(two_away), next_own, other_core(next_own)]
    sums = tiles(middle, col, rates, sums, False)
    next_other = after(next_other, middle[1], 0)
    part = tiles([next_other, other_core(next_other)], col, rates, sums, True)
    parts = lax.all_to_all(part.reshape(n_col, quarter, width), "col", 0, 0, tiled=True)
    grad = summed(parts)
    grad = lax.all_gather(grad, "tensor", axis=0, tiled=True)
    return result(grad, w_proj)


def solution(mesh):
    in_specs = (P(("row", "col"), "tensor"), P("tensor", None), P(("row", "col")), P())
    out_specs = P(("row", "col"), "tensor")
    return jax.shard_map(shards, mesh=mesh, in_specs=in_specs, out_specs=out_specs, check_vma=False)
```
